128 devices in a mesh: tm: 8 (over x, core), space: 16 (over z, y).
Axes of the slice: x: 4, y: 4, z: 4, core: 2. Of those that a mesh axis runs over, the one named last changes fastest.
Arguments:
- pixels: bfloat16 [327680, 128], P(('tm', 'space')), may hold values from -48 to 48
- weights: bfloat16 [327680], P(('tm', 'space')), may hold values from 0.5 to 2
- tile_index: int32 [327680], P(('tm', 'space')), may hold values from 0 to 15, as said below
- tile_row: int32 [327680], P(('tm', 'space')), may hold values from 0 to 159, as said below
- granule_day: int32 [327680], P(('tm', 'space')), may hold values from 0 to 63
Outputs:
- field: bfloat16 [16, 160, 512, 128], P('space', 'tm')
- basis: bfloat16 [16, 160, 256, 128], P('space', 'tm')
- propagator: float32 [256, 256], replicated
The draws below stay inside these ranges and needn't reach their ends.
Inputs may be any that keep to these rules, and one draw needn't show every extreme that they name: `tile_index`: of the rows of one device, at most 320 name one tile, and in every device's rows some tile is named by exactly 320. `tile_row`: of the rows of one device, at most 40 name one tile and a grid row from k * 20 to (k + 1) * 20 - 1 for one k, and in every device's rows some tile and k reach 40.
All inputs are finite; a program needn't handle non-finite values.
Results may differ from the reference program's by a relative error of at most 0.0061.
Values may be sent and summed in bfloat16 or wider, within the bound.
A program may use at most 64 MiB of HBM per device.

```python
import math
import jax
import jax.numpy as jnp
from jax import lax

PIX = 128
GR_DEV = 160
DAYS = 512
RANK = 256
ITERS = 8
DAY_DEV = 64
SW_DEV = 2560
SW_TM = 40960
SWATH = 327680
CAP = 320
CELLS = 327680
N_TM = 8
N_SPACE = 16


def swath_layout(key):
    blocks = SWATH // SW_DEV
    rows_tm = GR_DEV // N_TM

    def one_block(block_key):
        keys = jax.random.split(block_key, 6)
        hottest = jax.random.randint(keys[0], (), 0, N_SPACE)
        second = (hottest + jax.random.randint(keys[1], (), 1, N_SPACE)) % N_SPACE
        extra = jax.random.randint(keys[2], (), 0, CAP // 2)
        places = jnp.arange(SW_DEV, dtype=jnp.int32)
        rest = jnp.maximum(places - CAP - extra, 0)
        cycled = (hottest + 1 + rest % (N_SPACE - 1)) % N_SPACE
        tiles = jnp.where(places < CAP, hottest, jnp.where(places < CAP + extra, second, cycled))
        rest_rank = rest // (N_SPACE - 1) + jnp.where(cycled == second, extra, 0)
        order_rank = jnp.where(places < CAP, places, jnp.where(places < CAP + extra, places - CAP, rest_rank))
        rows = order_rank % N_TM * rows_tm + jax.random.randint(keys[3], (SW_DEV,), 0, rows_tm)
        days = jax.random.randint(keys[4], (SW_DEV,), 0, DAYS // N_TM)
        shuffle = jax.random.permutation(keys[5], SW_DEV)
        return (tiles[shuffle], rows[shuffle], days[shuffle])
    tiles, rows, days = jax.vmap(one_block)(jax.random.split(key, blocks))
    return (tiles.reshape(-1).astype(jnp.int32), rows.reshape(-1).astype(jnp.int32), days.reshape(-1).astype(jnp.int32))


def draw_tile_index(key, part):
    return swath_layout(jax.random.fold_in(key, 7))[0]


def draw_tile_row(key, part):
    return swath_layout(jax.random.fold_in(key, 7))[1]


def draw_granule_day(key, part):
    return swath_layout(jax.random.fold_in(key, 7))[2]


def draw_pixels(key, part):
    tiles, rows, days = swath_layout(jax.random.fold_in(key, 7))
    keys = jax.random.split(jax.random.fold_in(key, 11), 6)
    grid_rows = N_SPACE * GR_DEV
    cell_row = tiles * GR_DEV + rows
    global_day = jnp.arange(SWATH, dtype=jnp.int32) // SW_TM * (DAYS // N_TM) + days
    row_scale = jnp.exp(jax.random.uniform(keys[0], (grid_rows,), jnp.float32, 0.0, math.log(10.0)))
    common = 0.7
    noise = jnp.clip(jax.random.normal(keys[1], (SWATH, PIX), jnp.float32), -6.0, 6.0)
    mode_row = jnp.clip(jax.random.normal(keys[2], (grid_rows,), jnp.float32), -4.0, 4.0)
    mode_pix = jnp.clip(jax.random.normal(keys[3], (PIX,), jnp.float32), -4.0, 4.0)
    phase = jax.random.uniform(keys[4], (), jnp.float32, -math.pi, math.pi)
    day_noise = jnp.clip(jax.random.normal(keys[5], (DAYS,), jnp.float32), -4.0, 4.0)
    day_values = jnp.cos(2.0 * math.pi * jnp.arange(DAYS, dtype=jnp.float32) / 365.0 + phase) + 0.5 * day_noise
    mode_day = day_values[global_day]
    inner = common * mode_row[cell_row][:, None] * mode_pix[None, :] * mode_day[:, None] + noise
    inner = jnp.clip(inner, -8.0, 8.0)
    rise = 1.0 + 2.0 * tiles.astype(jnp.float32) / (N_SPACE - 1)
    values = row_scale[cell_row][:, None] * rise[:, None] * inner / 5.0
    return values.astype(jnp.bfloat16)


def shard_levels(key, shape, pieces, least, top_value):
    loudness = 1.0
    for axis_at, parts in pieces:
        heights = jax.random.uniform(jax.random.fold_in(jax.random.fold_in(key, 6), axis_at), (parts,), jnp.float32, least / len(pieces), top_value / len(pieces))
        loudness = loudness * jnp.repeat(jnp.exp(heights), shape[axis_at] // parts).reshape((-1,) + (1,) * (len(shape) - 1 - axis_at))
    return loudness


def setup_inputs(seed: int = 0) -> dict:
    seeds = jax.random.split(jax.random.key(seed), 6)
    pixels = draw_pixels(jax.random.fold_in(seeds[5], 71), 0)
    weights = jnp.clip(jnp.exp(math.log(2.0) - 1.3862944 * jax.random.uniform(seeds[1], (SWATH,), jnp.float32) ** shard_levels(seeds[1], (SWATH,), ((0, 128),), -0.2, 0.2)), 0.5, 2.0).astype(jnp.bfloat16)
    tile_index = draw_tile_index(jax.random.fold_in(seeds[5], 71), 0)
    tile_row = draw_tile_row(jax.random.fold_in(seeds[5], 71), 0)
    granule_day = draw_granule_day(jax.random.fold_in(seeds[5], 71), 0)
    return {"pixels": pixels, "weights": weights, "tile_index": tile_index, "tile_row": tile_row, "granule_day": granule_day}


def reference(pixels, weights, tile_index, tile_row, granule_day):
    swath = pixels.shape[0]
    gday = jnp.arange(swath, dtype=jnp.int32) // SW_TM * DAY_DEV + granule_day
    contrib = weights.astype(jnp.float32)[:, None] * pixels.astype(jnp.float32)
    target = tile_row * DAYS + gday

    def one_tile(which):
        place = jnp.where(tile_index == which, target, GR_DEV * DAYS)
        summed = jnp.zeros((GR_DEV * DAYS, PIX), jnp.float32).at[place].add(contrib, mode='drop')
        return summed.astype(jnp.bfloat16).reshape(GR_DEV, DAYS, PIX)
    field = lax.map(one_tile, jnp.arange(N_SPACE, dtype=jnp.int32))

    def add_tile(total, piece):
        values = piece.astype(jnp.float32)
        return (total + jnp.einsum('rdp,rep->de', values, values, precision=lax.Precision.HIGHEST), None)
    gram, _ = lax.scan(add_tile, jnp.zeros((DAYS, DAYS), jnp.float32), field)
    factor = jnp.linalg.cholesky(gram).T
    cross = jnp.dot(factor[:RANK, 1:], factor[:RANK, :-1].T, precision=lax.Precision.HIGHEST)
    polar = cross / jnp.sqrt(jnp.sum(cross * cross) + 1e-06)
    for sweep in range(ITERS):
        square = jnp.dot(polar.T, polar, precision=lax.Precision.HIGHEST)
        polar = 1.5 * polar - 0.5 * jnp.dot(polar, square, precision=lax.Precision.HIGHEST)
    propagator = jnp.sqrt(jnp.float32(RANK)) * polar
    inverse = lax.linalg.triangular_solve(factor[:RANK, :RANK], jnp.eye(RANK, dtype=factor.dtype), left_side=True, lower=False)
    scaled_inverse = (jnp.sqrt(jnp.float32(CELLS)) * inverse).astype(jnp.bfloat16).astype(jnp.float32)

    def project(piece):
        values = piece[:, :RANK, :].astype(jnp.float32)
        return jnp.einsum('rdp,dk->rkp', values, scaled_inverse, precision=lax.Precision.HIGHEST).astype(jnp.bfloat16)
    basis = lax.map(project, field)
    return (field, basis, propagator)
```

```python
import math

import jax
import jax.numpy as jnp
from jax import lax
from jax.experimental import pallas as pl
from jax.experimental.pallas import tpu as pltpu
from jax.sharding import PartitionSpec as P

MESH = pl.DeviceIdType.MESH
GR_DEV = 160
DAYS = 512
RANK = 256
ITERS = 8
PIX = 128
N_TM = 8
N_SPACE = 16
N_DEV = N_TM * N_SPACE
ROWS = 2560
BLOCKS = ROWS // PIX
GRID_ROWS = GR_DEV // N_TM
DAY_DEV = DAYS // N_TM
CAP = 40
SLOT = 48
KDIM = N_SPACE * SLOT
CELLS = N_SPACE * GR_DEV * PIX
VMEM_LIMIT = 50 * 1024 * 1024
F32 = jnp.float32
BF16 = jnp.bfloat16


def nt(a, b, precision=None):
    return lax.dot_general(a, b, (((1,), (1,)), ((), ())), precision=precision, preferred_element_type=F32)


def tn(a, b, precision=None):
    return lax.dot_general(a, b, (((0,), (0,)), ((), ())), precision=precision, preferred_element_type=F32)


def nn(a, b, precision=None):
    return lax.dot_general(a, b, (((1,), (0,)), ((), ())), precision=precision, preferred_element_type=F32)


def pack_kernel(pix_ref, w_ref, tile_ref, row_ref, day_ref, out_ref, pos_v, pos_s, src, buf, sem):
    sub = lax.broadcasted_iota(jnp.int32, (PIX, PIX), 0)
    lane = lax.broadcasted_iota(jnp.int32, (PIX, PIX), 1)
    ahead = jnp.concatenate([jnp.where(sub < lane, 1.0, 0.0), jnp.ones((PIX, PIX), F32)], axis=1).astype(BF16)
    is_w = sub < CAP
    is_row = sub < 2 * CAP
    slot = jnp.where(is_w, sub, jnp.where(is_row, sub - CAP, sub - 2 * CAP))
    running = jnp.zeros((PIX, PIX), F32)
    meta = jnp.zeros((PIX, PIX), F32)
    weights = w_ref[...].astype(F32)
    part = (row_ref[...] * 3277) >> 16
    dest_all = part * N_SPACE + tile_ref[...]
    row_all = (row_ref[...] - part * GRID_ROWS).astype(F32)
    day_all = day_ref[...].astype(F32)
    for b in range(BLOCKS):
        dest = dest_all[b : b + 1, :]
        hit = sub == dest
        onehot = jnp.where(hit, 1.0, 0.0).astype(BF16)
        counts = nn(onehot, ahead)
        before = counts[:, :PIX] + running
        running = running + counts[:, PIX:]
        rank = jnp.sum(jnp.where(hit, before, 0.0), axis=0, keepdims=True).astype(jnp.int32)
        value = jnp.where(is_w, weights[b : b + 1, :], jnp.where(is_row, row_all[b : b + 1, :], day_all[b : b + 1, :]))
        column = jnp.where(slot == rank, value, 0.0).astype(BF16)
        meta = meta + nt(onehot, column)
        pos_v[b : b + 1, :] = dest * SLOT + rank
    copy = pltpu.make_async_copy(pos_v, pos_s, sem)
    copy.start()
    src[...] = pix_ref[...].astype(F32)
    buf[...] = jnp.zeros_like(buf)
    copy.wait()

    def block(b, carry):
        def some(i, carry):
            for u in range(16):
                at = pos_s[b, i * 16 + u]
                buf[pl.ds(at, 1), :] = src[pl.ds(b * PIX + i * 16 + u, 1), :]
            return carry

        return lax.fori_loop(0, PIX // 16, some, carry)

    lax.fori_loop(0, BLOCKS, block, 0)
    buf[pl.ds(CAP, N_DEV, stride=SLOT), :] = meta

    def finish(i, carry):
        for u in range(4):
            d = i * 4 + u
            out_ref[d] = buf[pl.ds(pl.multiple_of(d * SLOT, 8), SLOT), :].astype(BF16)
        return carry

    lax.fori_loop(0, N_DEV // 4, finish, 0)


def pack(pixels, weights, tile, row, day):
    vm = pl.BlockSpec(memory_space=pltpu.VMEM)
    return pl.pallas_call(
        pack_kernel,
        name="pack_rows",
        out_shape=jax.ShapeDtypeStruct((N_DEV, SLOT, PIX), BF16),
        in_specs=[vm] * 5,
        out_specs=vm,
        scratch_shapes=[
            pltpu.VMEM((BLOCKS, PIX), jnp.int32),
            pltpu.SMEM((BLOCKS, PIX), jnp.int32),
            pltpu.VMEM((ROWS, PIX), F32),
            pltpu.VMEM((N_DEV * SLOT, PIX), F32),
            pltpu.SemaphoreType.DMA,
        ],
        compiler_params=pltpu.CompilerParams(vmem_limit_bytes=VMEM_LIMIT),
    )(pixels, *(a.reshape(BLOCKS, PIX) for a in (weights, tile, row, day)))


def me_and_peer():
    me = lax.axis_index("tm") * N_SPACE + lax.axis_index("space")

    def peer(j):
        other = lax.rem(me + j, N_DEV)
        return other, (other // N_SPACE, lax.rem(other, N_SPACE))

    return me, peer


def greet_all(peer):
    barrier = pltpu.get_barrier_semaphore()

    def greet(j, carry):
        pl.semaphore_signal(barrier, inc=1, device_id=peer(j)[1], device_id_type=MESH)
        return carry

    lax.fori_loop(1, N_DEV, greet, 0)
    pl.semaphore_wait(barrier, N_DEV - 1)


def exchange_kernel(x_ref, o_ref, send_sem, recv_sem, own_sem):
    me, peer = me_and_peer()
    own = pltpu.make_async_copy(x_ref.at[me], o_ref.at[me], own_sem)
    own.start()
    greet_all(peer)

    def send(j, carry):
        other, device = peer(j)
        pltpu.make_async_remote_copy(
            src_ref=x_ref.at[other],
            dst_ref=o_ref.at[me],
            send_sem=send_sem,
            recv_sem=recv_sem,
            device_id=device,
            device_id_type=MESH,
        ).start()
        return carry

    lax.fori_loop(1, N_DEV, send, 0)
    own.wait()
    all_of_it = pltpu.make_async_remote_copy(
        src_ref=x_ref.at[pl.ds(0, N_DEV - 1)],
        dst_ref=o_ref.at[pl.ds(0, N_DEV - 1)],
        send_sem=send_sem,
        recv_sem=recv_sem,
        device_id=peer(1)[1],
        device_id_type=MESH,
    )
    all_of_it.wait_send()
    all_of_it.wait_recv()


def exchange(packed):
    vm = pl.BlockSpec(memory_space=pltpu.VMEM)
    return pl.pallas_call(
        exchange_kernel,
        name="exchange_rows",
        out_shape=jax.ShapeDtypeStruct((N_DEV, SLOT, PIX), BF16),
        in_specs=[vm],
        out_specs=vm,
        scratch_shapes=[pltpu.SemaphoreType.DMA, pltpu.SemaphoreType.DMA, pltpu.SemaphoreType.DMA],
        compiler_params=pltpu.CompilerParams(collective_id=0, has_side_effects=True, vmem_limit_bytes=VMEM_LIMIT),
    )(packed)


def sum_kernel(x_ref, o_ref, parts, total, send_sem, recv_sem, send2, recv2, own_sem):
    me, peer = me_and_peer()
    greet_all(peer)

    def scatter(j, carry):
        other, device = peer(j)
        pltpu.make_async_remote_copy(
            src_ref=x_ref.at[other],
            dst_ref=parts.at[me],
            send_sem=send_sem,
            recv_sem=recv_sem,
            device_id=device,
            device_id_type=MESH,
        ).start()
        return carry

    lax.fori_loop(1, N_DEV, scatter, 0)
    own = pltpu.make_async_copy(x_ref.at[me], parts.at[me], own_sem)
    own.start()
    own.wait()
    scattered = pltpu.make_async_remote_copy(
        src_ref=x_ref.at[pl.ds(0, N_DEV - 1)],
        dst_ref=parts.at[pl.ds(0, N_DEV - 1)],
        send_sem=send_sem,
        recv_sem=recv_sem,
        device_id=peer(1)[1],
        device_id_type=MESH,
    )
    scattered.wait_recv()
    total[...] = jnp.sum(parts[...], axis=0)

    def spread(j, carry):
        pltpu.make_async_remote_copy(
            src_ref=total,
            dst_ref=o_ref.at[me],
            send_sem=send2,
            recv_sem=recv2,
            device_id=peer(j)[1],
            device_id_type=MESH,
        ).start()
        return carry

    lax.fori_loop(1, N_DEV, spread, 0)
    own = pltpu.make_async_copy(total, o_ref.at[me], own_sem)
    own.start()
    own.wait()
    scattered.wait_send()
    gathered = pltpu.make_async_remote_copy(
        src_ref=parts.at[pl.ds(0, N_DEV - 1)],
        dst_ref=o_ref.at[pl.ds(0, N_DEV - 1)],
        send_sem=send2,
        recv_sem=recv2,
        device_id=peer(1)[1],
        device_id_type=MESH,
    )
    gathered.wait_send()
    gathered.wait_recv()


def sum_over_devices(chunks):
    vm = pl.BlockSpec(memory_space=pltpu.VMEM)
    return pl.pallas_call(
        sum_kernel,
        name="sum_gram",
        out_shape=jax.ShapeDtypeStruct((N_DEV, 8, PIX), F32),
        in_specs=[vm],
        out_specs=vm,
        scratch_shapes=[pltpu.VMEM((N_DEV, 8, PIX), F32), pltpu.VMEM((8, PIX), F32)] + [pltpu.SemaphoreType.DMA] * 5,
        compiler_params=pltpu.CompilerParams(collective_id=1, has_side_effects=True, vmem_limit_bytes=VMEM_LIMIT),
    )(chunks)


G_STEP = 10


def grid_kernel(recv_ref, field_ref, gram_ref, meta_s, w_s, t_s, onehot_s, flat_s):
    meta_s[...] = recv_ref[:, SLOT - 16 :, :].astype(F32)[:, 8:, :].reshape(N_DEV * 8, PIX)
    meta = meta_s[pl.ds(0, N_DEV, stride=8), :].astype(BF16)
    lab = lax.broadcasted_iota(jnp.int32, (PIX, KDIM), 0)
    col = lax.broadcasted_iota(jnp.int32, (PIX, KDIM), 1)
    at = col - SLOT * ((col * 1366) >> 16)
    used = at < CAP
    pick_w = jnp.where(used & (lab == at), 1.0, 0.0).astype(BF16)
    pick_t = (
        jnp.where(used & (lab == at + CAP), float(DAY_DEV), 0.0) + jnp.where(used & (lab == at + 2 * CAP), 1.0, 0.0)
    ).astype(BF16)
    from_src = (lax.broadcasted_iota(jnp.int32, (N_SPACE, KDIM), 1) * 1366) >> 16
    mine = from_src == lax.broadcasted_iota(jnp.int32, (N_SPACE, KDIM), 0)
    w_all = nn(meta, pick_w)
    t_all = nn(meta, pick_t)
    for i in range(N_TM):
        rows = slice(i * N_SPACE, (i + 1) * N_SPACE)
        w_s[i : i + 1, :] = jnp.sum(jnp.where(mine, w_all[rows], 0.0), axis=0, keepdims=True)
        t_s[i : i + 1, :] = jnp.sum(jnp.where(mine, t_all[rows], 0.0), axis=0, keepdims=True)

    day = lax.broadcasted_iota(jnp.int32, (DAY_DEV, KDIM), 0).astype(F32)

    def one(i, carry):
        w_row = w_s[pl.ds(i, 1), :]
        t_row = t_s[pl.ds(i, 1), :]
        pix = recv_ref[pl.ds(pl.multiple_of(i * N_SPACE, N_SPACE), N_SPACE)].reshape(KDIM, PIX)
        days = pl.ds(pl.multiple_of(i * DAY_DEV, DAY_DEV), DAY_DEV)
        for half in range(GRID_ROWS // G_STEP):
            for u in range(G_STEP):
                g = half * G_STEP + u
                onehot_s[u * DAY_DEV : (u + 1) * DAY_DEV, :] = jnp.where(
                    day == t_row - float(g * DAY_DEV), w_row, 0.0
                ).astype(BF16)
            cells = nn(onehot_s[...], pix).astype(BF16)
            for u in range(G_STEP):
                g = half * G_STEP + u
                block = cells[u * DAY_DEV : (u + 1) * DAY_DEV, :]
                field_ref[g, days, :] = block
                flat_s[days, g * PIX : (g + 1) * PIX] = block
        return carry

    lax.fori_loop(0, N_TM, one, 0)
    gram = nt(flat_s[:RANK, :], flat_s[...])
    for q in range(DAYS // PIX):
        gram_ref[q * (RANK // 8) : (q + 1) * (RANK // 8)] = gram[:, q * PIX : (q + 1) * PIX].reshape(RANK // 8, 8, PIX)


def to_grid(received):
    vm = pl.BlockSpec(memory_space=pltpu.VMEM)
    return pl.pallas_call(
        grid_kernel,
        name="grid_and_gram",
        out_shape=(
            jax.ShapeDtypeStruct((GRID_ROWS, DAYS, PIX), BF16),
            jax.ShapeDtypeStruct((N_DEV, 8, PIX), F32),
        ),
        in_specs=[vm],
        out_specs=(vm, vm),
        scratch_shapes=[
            pltpu.VMEM((N_DEV * 8, PIX), F32),
            pltpu.VMEM((N_TM, KDIM), F32),
            pltpu.VMEM((N_TM, KDIM), F32),
            pltpu.VMEM((G_STEP * DAY_DEV, KDIM), BF16),
            pltpu.VMEM((DAYS, GRID_ROWS * PIX), BF16),
        ],
        compiler_params=pltpu.CompilerParams(vmem_limit_bytes=VMEM_LIMIT),
    )(received)


PANEL = 32
HIGHEST = lax.Precision.HIGHEST


def split3(x):
    high = x.astype(BF16)
    rest = x - high.astype(F32)
    mid = rest.astype(BF16)
    return high, mid, (rest - mid.astype(F32)).astype(BF16)


def dense_kernel(gram_ref, field_ref, basis_ref, prop_ref, m_s, v_s):
    lane2 = lax.broadcasted_iota(jnp.int32, (RANK, RANK), 1)
    sub2 = lax.broadcasted_iota(jnp.int32, (RANK, RANK), 0)
    m_s[:, :PIX] = gram_ref[0]
    m_s[:, PIX:RANK] = gram_ref[1]
    m_s[:, RANK:] = jnp.where(lane2 == sub2, 1.0, 0.0)
    sub = lax.broadcasted_iota(jnp.int32, (PANEL, PIX), 0)

    def panel(p, carry):
        start = pl.multiple_of(p * PANEL, PANEL)
        rows = m_s[pl.ds(start, PANEL), :]
        turned = pltpu.roll(rows[:, :RANK], lax.rem(RANK - start, RANK), 1)
        pieces = [turned[:, :PIX]] + [rows[:, q * PIX : (q + 1) * PIX] for q in range(4)]
        scale = jnp.zeros((PANEL, PIX), F32)
        for q in range(PANEL // 8):
            cols = [jnp.broadcast_to(pieces[0][:, q * 8 + k : q * 8 + k + 1], (PANEL, PIX)) for k in range(8)]
            for k in range(8):
                j = q * 8 + k
                pivot = cols[k][j : j + 1, :]
                factor = jnp.where(sub > j, cols[k] * (1.0 / pivot), 0.0)
                scale = jnp.where(sub == j, lax.rsqrt(pivot), scale)
                for kk in range(k + 1, 8):
                    cols[kk] = cols[kk] - factor * cols[kk][j : j + 1, :]
                pieces = [x - factor * x[j : j + 1, :] for x in pieces]
        done = jnp.concatenate([x * scale for x in pieces[1:]], axis=1)
        v_s[pl.ds(start, PANEL), :] = done
        high, mid, low = split3(done)
        left = jnp.concatenate([high, high, mid, mid, high, low], axis=0)[:, :RANK]
        right = jnp.concatenate([high, mid, high, mid, low, high], axis=0)
        m_s[...] = m_s[...] - tn(left, right)
        return carry

    lax.fori_loop(0, RANK // PANEL, panel, 0)
    inv = v_s[:, RANK:]
    scaled = (math.sqrt(CELLS) * inv).astype(BF16)
    for g in range(0, GRID_ROWS, 2):
        both = nn(scaled, jnp.concatenate([field_ref[g], field_ref[g + 1]], axis=1)).astype(BF16)
        basis_ref[g] = both[:, :PIX]
        basis_ref[g + 1] = both[:, PIX:]
    first = jnp.where(lane2 >= sub2, v_s[:, :RANK], 0.0)
    second = nn(inv, jnp.concatenate([gram_ref[2], gram_ref[3]], axis=1), HIGHEST)
    factor = jnp.concatenate([first, second], axis=1)
    last = lax.broadcasted_iota(jnp.int32, (RANK, DAYS), 1) == DAYS - 1
    later = jnp.where(last, 0.0, pltpu.roll(factor, DAYS - 1, 1))
    cross = nt(later, factor, HIGHEST)
    polar = cross * (1.0 / jnp.sqrt(jnp.sum(cross * cross) + 1e-06))

    def sweep(i, polar):
        square = nt(polar, polar, HIGHEST)
        return 1.5 * polar - 0.5 * nn(square, polar, HIGHEST)

    polar = lax.fori_loop(0, ITERS, sweep, polar)
    prop_ref[...] = math.sqrt(RANK) * polar


def dense(gram, field):
    vm = pl.BlockSpec(memory_space=pltpu.VMEM)
    return pl.pallas_call(
        dense_kernel,
        name="dense_algebra",
        grid=(1,),
        out_shape=(
            jax.ShapeDtypeStruct((GRID_ROWS, RANK, PIX), BF16),
            jax.ShapeDtypeStruct((RANK, RANK), F32),
        ),
        in_specs=[
            pl.BlockSpec((DAYS // PIX, RANK, PIX), lambda i: (0, 0, 0)),
            pl.BlockSpec((GRID_ROWS, RANK, PIX), lambda i: (0, 0, 0)),
        ],
        out_specs=(
            pl.BlockSpec((GRID_ROWS, RANK, PIX), lambda i: (0, 0, 0)),
            pl.BlockSpec((RANK, RANK), lambda i: (0, 0)),
        ),
        scratch_shapes=[pltpu.VMEM((RANK, DAYS), F32), pltpu.VMEM((RANK, DAYS), F32)],
        compiler_params=pltpu.CompilerParams(vmem_limit_bytes=VMEM_LIMIT),
    )(gram.reshape(DAYS // PIX, RANK, PIX), field)


def body(pixels, weights, tile_index, tile_row, granule_day):
    packed = pack(pixels, weights, tile_index, tile_row, granule_day)
    received = exchange(packed)
    field, chunks = to_grid(received)
    gram = sum_over_devices(chunks)
    basis, propagator = dense(gram, field)
    return (field[None], basis[None], propagator)


def solution(mesh):
    split = P(("tm", "space"))
    return jax.shard_map(
        body,
        mesh=mesh,
        in_specs=(P(("tm", "space"), None), split, split, split, split),
        out_specs=(P("space", "tm", None, None), P("space", "tm", None, None), P()),
        check_vma=False,
    )
```

```python
import math

import jax
import jax.numpy as jnp
from jax import lax
from jax.experimental import pallas as pl
from jax.experimental.pallas import tpu as pltpu
from jax.sharding import PartitionSpec as P

MESH = pl.DeviceIdType.MESH
GR_DEV = 160
DAYS = 512
RANK = 256
ITERS = 8
PIX = 128
N_TM = 8
N_SPACE = 16
N_DEV = N_TM * N_SPACE
ROWS = 2560
BLOCKS = ROWS // PIX
GRID_ROWS = GR_DEV // N_TM
DAY_DEV = DAYS // N_TM
CAP = 40
SLOT = 48
KDIM = N_SPACE * SLOT
CELLS = N_SPACE * GR_DEV * PIX
VMEM_LIMIT = 62 * 1024 * 1024 + 512 * 1024
F32 = jnp.float32
BF16 = jnp.bfloat16


def nt(a, b, precision=None):
    return lax.dot_general(a, b, (((1,), (1,)), ((), ())), precision=precision, preferred_element_type=F32)


def tn(a, b, precision=None):
    return lax.dot_general(a, b, (((0,), (0,)), ((), ())), precision=precision, preferred_element_type=F32)


def nn(a, b, precision=None):
    return lax.dot_general(a, b, (((1,), (0,)), ((), ())), precision=precision, preferred_element_type=F32)


def pack_kernel(
    pix_hbm, w_hbm, tile_hbm, row_hbm, day_hbm, out_hbm,
    pix_ref, w_ref, tile_ref, row_ref, day_ref, pos_v, pos_s, src, buf, out_ref, sem, in_sems, out_sems,
):
    loads = [
        pltpu.make_async_copy(a, b, in_sems.at[n])
        for n, (a, b) in enumerate(
            ((row_hbm, row_ref), (tile_hbm, tile_ref), (day_hbm, day_ref), (w_hbm, w_ref), (pix_hbm, pix_ref))
        )
    ]
    for load in loads:
        load.start()
    buf[...] = jnp.zeros_like(buf)
    sub = lax.broadcasted_iota(jnp.int32, (PIX, PIX), 0)
    lane = lax.broadcasted_iota(jnp.int32, (PIX, PIX), 1)
    ahead = jnp.concatenate([jnp.where(sub < lane, 1.0, 0.0), jnp.ones((PIX, PIX), F32)], axis=1).astype(BF16)
    is_w = sub < CAP
    is_row = sub < 2 * CAP
    slot = jnp.where(is_w, sub, jnp.where(is_row, sub - CAP, sub - 2 * CAP))
    for load in loads[:-1]:
        load.wait()
    running = jnp.zeros((PIX, PIX), F32)
    meta = jnp.zeros((PIX, PIX), F32)
    weights = w_ref[...].astype(F32)
    part = (row_ref[...] * 3277) >> 16
    dest_all = part * N_SPACE + tile_ref[...]
    row_all = (row_ref[...] - part * GRID_ROWS).astype(F32)
    day_all = day_ref[...].astype(F32)
    for b in range(BLOCKS):
        dest = dest_all[b : b + 1, :]
        hit = sub == dest
        onehot = jnp.where(hit, 1.0, 0.0).astype(BF16)
        counts = nn(onehot, ahead)
        before = counts[:, :PIX] + running
        running = running + counts[:, PIX:]
        rank = jnp.sum(jnp.where(hit, before, 0.0), axis=0, keepdims=True).astype(jnp.int32)
        value = jnp.where(is_w, weights[b : b + 1, :], jnp.where(is_row, row_all[b : b + 1, :], day_all[b : b + 1, :]))
        column = jnp.where(slot == rank, value, 0.0).astype(BF16)
        meta = meta + nt(onehot, column)
        pos_v[b : b + 1, :] = dest * SLOT + rank
    copy = pltpu.make_async_copy(pos_v, pos_s, sem)
    copy.start()
    loads[-1].wait()
    src[...] = pix_ref[...].astype(F32)
    copy.wait()

    def block(b, carry):
        def some(i, carry):
            for u in range(16):
                at = pos_s[b, i * 16 + u]
                buf[pl.ds(at, 1), :] = src[pl.ds(b * PIX + i * 16 + u, 1), :]
            return carry

        return lax.fori_loop(0, PIX // 16, some, carry)

    lax.fori_loop(0, BLOCKS, block, 0)
    buf[pl.ds(CAP, N_DEV, stride=SLOT), :] = meta

    leaving = []
    for part in range(N_TM):
        blocks = pl.ds(part * N_SPACE, N_SPACE)
        rows = buf[part * KDIM : (part + 1) * KDIM, :]
        out_ref[blocks] = rows.astype(BF16).reshape(N_SPACE, SLOT, PIX)
        leaving.append(pltpu.make_async_copy(out_ref.at[blocks], out_hbm.at[blocks], out_sems.at[part]))
        leaving[-1].start()
    for copy in leaving:
        copy.wait()


def pack(pixels, weights, tile, row, day):
    hbm = pl.BlockSpec(memory_space=pltpu.HBM)
    return pl.pallas_call(
        pack_kernel,
        name="pack_rows",
        out_shape=jax.ShapeDtypeStruct((N_DEV, SLOT, PIX), BF16),
        in_specs=[hbm] * 5,
        out_specs=hbm,
        scratch_shapes=[
            pltpu.VMEM((ROWS, PIX), BF16),
            pltpu.VMEM((BLOCKS, PIX), BF16),
            pltpu.VMEM((BLOCKS, PIX), jnp.int32),
            pltpu.VMEM((BLOCKS, PIX), jnp.int32),
            pltpu.VMEM((BLOCKS, PIX), jnp.int32),
            pltpu.VMEM((BLOCKS, PIX), jnp.int32),
            pltpu.SMEM((BLOCKS, PIX), jnp.int32),
            pltpu.VMEM((ROWS, PIX), F32),
            pltpu.VMEM((N_DEV * SLOT, PIX), F32),
            pltpu.VMEM((N_DEV, SLOT, PIX), BF16),
            pltpu.SemaphoreType.DMA,
            pltpu.SemaphoreType.DMA((5,)),
            pltpu.SemaphoreType.DMA((N_TM,)),
        ],
        compiler_params=pltpu.CompilerParams(vmem_limit_bytes=VMEM_LIMIT),
    )(pixels, *(a.reshape(BLOCKS, PIX) for a in (weights, tile, row, day)))


def me_and_peer():
    me = lax.axis_index("tm") * N_SPACE + lax.axis_index("space")

    def peer(j):
        other = lax.rem(me + j, N_DEV)
        return other, (other // N_SPACE, lax.rem(other, N_SPACE))

    return me, peer


def greet_all(peer):
    barrier = pltpu.get_barrier_semaphore()

    def greet(j, carry):
        pl.semaphore_signal(barrier, inc=1, device_id=peer(j)[1], device_id_type=MESH)
        return carry

    lax.fori_loop(1, N_DEV, greet, 0)
    pl.semaphore_wait(barrier, N_DEV - 1)


G_STEP = 10
HALF = N_DEV // 2


def remote(src, dst, send_sem, recv_sem, device):
    return pltpu.make_async_remote_copy(
        src_ref=src, dst_ref=dst, send_sem=send_sem, recv_sem=recv_sem, device_id=device, device_id_type=MESH
    )


def exchange_kernel(
    x_ref, field_ref, gram_ref, recv, meta_s, onehot_s, flat_s, part_s, pair_s, tiles_s, total_s,
    send_sem, recv_sem, sum_send, sum_recv, out_sems,
):
    tm, space = lax.axis_index("tm"), lax.axis_index("space")
    me, peer = me_and_peer()
    own = pltpu.make_async_copy(x_ref.at[me], recv.at[me], recv_sem.at[0])
    own.start()
    greet_all(peer)

    def send(j, carry):
        stage = j // N_SPACE
        to_tm = lax.rem(tm + stage, N_TM)
        to_space = lax.rem(space + lax.rem(j, N_SPACE), N_SPACE)
        remote(
            x_ref.at[to_tm * N_SPACE + to_space], recv.at[me], send_sem, recv_sem.at[stage], (to_tm, to_space)
        ).start()
        return carry

    lax.fori_loop(1, N_DEV, send, 0)

    lab = lax.broadcasted_iota(jnp.int32, (PIX, KDIM), 0)
    col = lax.broadcasted_iota(jnp.int32, (PIX, KDIM), 1)
    at = col - SLOT * ((col * 1366) >> 16)
    used = at < CAP
    pick_w = jnp.where(used & (lab == at), 1.0, 0.0).astype(BF16)
    pick_t = (
        jnp.where(used & (lab == at + CAP), float(DAY_DEV), 0.0) + jnp.where(used & (lab == at + 2 * CAP), 1.0, 0.0)
    ).astype(BF16)
    from_src = (lax.broadcasted_iota(jnp.int32, (N_SPACE, KDIM), 1) * 1366) >> 16
    mine = from_src == lax.broadcasted_iota(jnp.int32, (N_SPACE, KDIM), 0)
    day = lax.broadcasted_iota(jnp.int32, (DAY_DEV, KDIM), 0).astype(F32)

    def take(stage, carry):
        i = lax.rem(tm + N_TM - stage, N_TM)
        blocks = pl.ds(pl.multiple_of(i * N_SPACE, N_SPACE), N_SPACE)
        remote(x_ref.at[pl.ds(0, N_SPACE)], recv.at[blocks], send_sem, recv_sem.at[stage], (tm, space)).wait_recv()
        meta_s[...] = recv[blocks, SLOT - 16 :, :].astype(F32)[:, 8:, :].reshape(N_SPACE * 8, PIX)
        meta = meta_s[pl.ds(0, N_SPACE, stride=8), :].astype(BF16)
        w_row = jnp.sum(jnp.where(mine, nn(meta, pick_w), 0.0), axis=0, keepdims=True)
        t_row = jnp.sum(jnp.where(mine, nn(meta, pick_t), 0.0), axis=0, keepdims=True)
        pix = recv[blocks].reshape(KDIM, PIX)
        days = pl.ds(pl.multiple_of(i * DAY_DEV, DAY_DEV), DAY_DEV)
        for half in range(GRID_ROWS // G_STEP):
            for u in range(G_STEP):
                g = half * G_STEP + u
                onehot_s[u * DAY_DEV : (u + 1) * DAY_DEV, :] = jnp.where(
                    day == t_row - float(g * DAY_DEV), w_row, 0.0
                ).astype(BF16)
            cells = nn(onehot_s[...], pix).astype(BF16)
            for u in range(G_STEP):
                g = half * G_STEP + u
                block = cells[u * DAY_DEV : (u + 1) * DAY_DEV, :]
                flat_s[days, g * PIX : (g + 1) * PIX] = block
        return carry

    lax.fori_loop(0, N_TM, take, 0)
    leaving = [
        pltpu.make_async_copy(flat_s.at[:, pl.ds(g * PIX, PIX)], field_ref.at[g], out_sems.at[g])
        for g in range(GRID_ROWS)
    ]

    core = lax.rem(tm, 2)
    chip = (tm // 2) * N_SPACE + space
    partner = (tm + 1 - 2 * core, space)

    def half_gram(which):
        rows = flat_s[pl.ds(pl.multiple_of(which * RANK, RANK), RANK), :]
        gram = nt(flat_s[:RANK, :], rows)
        return [gram[:, q * PIX : (q + 1) * PIX].reshape(RANK // 8, 8, PIX) for q in range(2)]

    given = half_gram(1 - core)
    part_s[: HALF // 2] = given[0]
    part_s[HALF // 2 :] = given[1]
    to_pair = remote(part_s, pair_s, sum_send.at[0], sum_recv.at[0], partner)
    to_pair.start()
    for copy in leaving:
        copy.start()
    kept = half_gram(core)
    to_pair.wait_recv()
    pair_s[: HALF // 2] = pair_s[: HALF // 2] + kept[0]
    pair_s[HALF // 2 :] = pair_s[HALF // 2 :] + kept[1]

    def other_chip(j):
        other = lax.rem(chip + j, HALF)
        return other, ((other // N_SPACE) * 2 + core, lax.rem(other, N_SPACE))

    def scatter(j, carry):
        other, device = other_chip(j)
        remote(pair_s.at[other], tiles_s.at[chip], sum_send.at[1], sum_recv.at[1], device).start()
        return carry

    lax.fori_loop(1, HALF, scatter, 0)
    tiles_s[chip] = pair_s[chip]
    scattered = remote(
        pair_s.at[pl.ds(0, HALF - 1)], tiles_s.at[pl.ds(0, HALF - 1)], sum_send.at[1], sum_recv.at[1], partner
    )
    scattered.wait_recv()
    total_s[...] = jnp.sum(tiles_s[...], axis=0)
    place = core * HALF + chip

    def spread(j, carry):
        remote(total_s, gram_ref.at[place], sum_send.at[2], sum_recv.at[2], other_chip(j)[1]).start()
        return carry

    lax.fori_loop(1, HALF, spread, 0)
    gram_ref[place] = total_s[...]
    gathered = remote(
        pair_s.at[pl.ds(0, HALF - 1)], tiles_s.at[pl.ds(0, HALF - 1)], sum_send.at[2], sum_recv.at[2], partner
    )
    gathered.wait_recv()
    my_half = gram_ref.at[pl.ds(core * HALF, HALF)]
    swap = remote(my_half, my_half, sum_send.at[3], sum_recv.at[3], partner)
    swap.start()
    remote(
        x_ref.at[pl.ds(0, N_DEV - 1)], recv.at[pl.ds(0, N_DEV - 1)], send_sem, recv_sem.at[0], partner
    ).wait_send()
    to_pair.wait_send()
    scattered.wait_send()
    gathered.wait_send()
    for copy in leaving:
        copy.wait()
    swap.wait()


def exchange(packed):
    vm = pl.BlockSpec(memory_space=pltpu.VMEM)
    tiles = pltpu.VMEM((HALF, 8, PIX), F32)
    return pl.pallas_call(
        exchange_kernel,
        name="exchange_grid_sum",
        out_shape=(
            jax.ShapeDtypeStruct((GRID_ROWS, DAYS, PIX), BF16),
            jax.ShapeDtypeStruct((N_DEV, 8, PIX), F32),
        ),
        in_specs=[pl.BlockSpec(memory_space=pltpu.HBM)],
        out_specs=(pl.BlockSpec(memory_space=pltpu.HBM), vm),
        scratch_shapes=[
            pltpu.VMEM((N_DEV, SLOT, PIX), BF16),
            pltpu.VMEM((N_SPACE * 8, PIX), F32),
            pltpu.VMEM((G_STEP * DAY_DEV, KDIM), BF16),
            pltpu.VMEM((DAYS, GRID_ROWS * PIX), BF16),
            tiles,
            tiles,
            tiles,
            pltpu.VMEM((8, PIX), F32),
            pltpu.SemaphoreType.DMA,
            pltpu.SemaphoreType.DMA((N_TM,)),
            pltpu.SemaphoreType.DMA((4,)),
            pltpu.SemaphoreType.DMA((4,)),
            pltpu.SemaphoreType.DMA((GRID_ROWS,)),
        ],
        compiler_params=pltpu.CompilerParams(collective_id=0, has_side_effects=True, vmem_limit_bytes=VMEM_LIMIT),
    )(packed)


PANEL = 32
HIGHEST = lax.Precision.HIGHEST


def split3(x):
    high = x.astype(BF16)
    rest = x - high.astype(F32)
    mid = rest.astype(BF16)
    return high, mid, (rest - mid.astype(F32)).astype(BF16)


def dense_kernel(gram_ref, field_in, field_out, basis_ref, prop_ref, m_s, v_s, field_ref, sems):
    arriving = pltpu.make_async_copy(field_in, field_ref, sems.at[0])
    arriving.start()
    leaving = pltpu.make_async_copy(field_ref, field_out, sems.at[1])
    lane2 = lax.broadcasted_iota(jnp.int32, (RANK, RANK), 1)
    sub2 = lax.broadcasted_iota(jnp.int32, (RANK, RANK), 0)
    m_s[:, :PIX] = gram_ref[0]
    m_s[:, PIX:RANK] = gram_ref[1]
    m_s[:, RANK:] = jnp.where(lane2 == sub2, 1.0, 0.0)
    sub = lax.broadcasted_iota(jnp.int32, (PANEL, PIX), 0)

    def panel(p, carry):
        start = pl.multiple_of(p * PANEL, PANEL)
        rows = m_s[pl.ds(start, PANEL), :]
        turned = pltpu.roll(rows[:, :RANK], lax.rem(RANK - start, RANK), 1)
        pieces = [turned[:, :PIX]] + [rows[:, q * PIX : (q + 1) * PIX] for q in range(4)]
        scale = jnp.zeros((PANEL, PIX), F32)
        for q in range(PANEL // 8):
            cols = [jnp.broadcast_to(pieces[0][:, q * 8 + k : q * 8 + k + 1], (PANEL, PIX)) for k in range(8)]
            for k in range(8):
                j = q * 8 + k
                pivot = cols[k][j : j + 1, :]
                factor = jnp.where(sub > j, cols[k] * (1.0 / pivot), 0.0)
                scale = jnp.where(sub == j, lax.rsqrt(pivot), scale)
                for kk in range(k + 1, 8):
                    cols[kk] = cols[kk] - factor * cols[kk][j : j + 1, :]
                pieces = [x - factor * x[j : j + 1, :] for x in pieces]
        done = jnp.concatenate([x * scale for x in pieces[1:]], axis=1)
        v_s[pl.ds(start, PANEL), :] = done
        high, mid, low = split3(done)
        left = jnp.concatenate([high, high, mid, mid, high, low], axis=0)[:, :RANK]
        right = jnp.concatenate([high, mid, high, mid, low, high], axis=0)
        m_s[...] = m_s[...] - tn(left, right)
        return carry

    lax.fori_loop(0, RANK // PANEL, panel, 0)
    inv = v_s[:, RANK:]
    scaled = (math.sqrt(CELLS) * inv).astype(BF16)
    arriving.wait()
    leaving.start()
    for g in range(0, GRID_ROWS, 2):
        both = nn(scaled, jnp.concatenate([field_ref[g, :RANK], field_ref[g + 1, :RANK]], axis=1)).astype(BF16)
        basis_ref[g] = both[:, :PIX]
        basis_ref[g + 1] = both[:, PIX:]
    first = jnp.where(lane2 >= sub2, v_s[:, :RANK], 0.0)
    second = nn(inv, jnp.concatenate([gram_ref[2], gram_ref[3]], axis=1), HIGHEST)
    factor = jnp.concatenate([first, second], axis=1)
    last = lax.broadcasted_iota(jnp.int32, (RANK, DAYS), 1) == DAYS - 1
    later = jnp.where(last, 0.0, pltpu.roll(factor, DAYS - 1, 1))
    cross = nt(later, factor, HIGHEST)
    polar = cross * (1.0 / jnp.sqrt(jnp.sum(cross * cross) + 1e-06))

    def sweep(i, polar):
        square = nt(polar, polar, HIGHEST)
        return 1.5 * polar - 0.5 * nn(square, polar, HIGHEST)

    polar = lax.fori_loop(0, ITERS, sweep, polar)
    prop_ref[...] = math.sqrt(RANK) * polar
    leaving.wait()


def dense(gram, field):
    vm = pl.BlockSpec(memory_space=pltpu.VMEM)
    hbm = pl.BlockSpec(memory_space=pltpu.HBM)
    return pl.pallas_call(
        dense_kernel,
        name="dense_algebra",
        out_shape=(
            jax.ShapeDtypeStruct((GRID_ROWS, DAYS, PIX), BF16),
            jax.ShapeDtypeStruct((GRID_ROWS, RANK, PIX), BF16),
            jax.ShapeDtypeStruct((RANK, RANK), F32),
        ),
        in_specs=[vm, hbm],
        out_specs=(hbm, vm, vm),
        scratch_shapes=[
            pltpu.VMEM((RANK, DAYS), F32),
            pltpu.VMEM((RANK, DAYS), F32),
            pltpu.VMEM((GRID_ROWS, DAYS, PIX), BF16),
            pltpu.SemaphoreType.DMA((2,)),
        ],
        compiler_params=pltpu.CompilerParams(vmem_limit_bytes=VMEM_LIMIT),
    )(gram.reshape(DAYS // PIX, RANK, PIX), field)


def body(pixels, weights, tile_index, tile_row, granule_day):
    packed = pack(pixels, weights, tile_index, tile_row, granule_day)
    field, gram = exchange(packed)
    field, basis, propagator = dense(gram, field)
    return (field[None], basis[None], propagator)


def solution(mesh):
    split = P(("tm", "space"))
    return jax.shard_map(
        body,
        mesh=mesh,
        in_specs=(P(("tm", "space"), None), split, split, split, split),
        out_specs=(P("space", "tm", None, None), P("space", "tm", None, None), P()),
        check_vma=False,
    )
```

```python
import math

import jax
import jax.numpy as jnp
from jax import lax
from jax.experimental import pallas as pl
from jax.experimental.pallas import tpu as pltpu
from jax.sharding import PartitionSpec as P

MESH = pl.DeviceIdType.MESH
GR_DEV = 160
DAYS = 512
RANK = 256
ITERS = 8
PIX = 128
N_TM = 8
N_SPACE = 16
N_DEV = N_TM * N_SPACE
ROWS = 2560
BLOCKS = ROWS // PIX
GRID_ROWS = GR_DEV // N_TM
DAY_DEV = DAYS // N_TM
CAP = 40
SLOT = 48
KDIM = N_SPACE * SLOT
CELLS = N_SPACE * GR_DEV * PIX
VMEM_LIMIT = 62 * 1024 * 1024 + 512 * 1024
F32 = jnp.float32
BF16 = jnp.bfloat16


def nt(a, b):
    return lax.dot_general(a, b, (((1,), (1,)), ((), ())), preferred_element_type=F32)


def tn(a, b):
    return lax.dot_general(a, b, (((0,), (0,)), ((), ())), preferred_element_type=F32)


def nn(a, b):
    return lax.dot_general(a, b, (((1,), (0,)), ((), ())), preferred_element_type=F32)


def pack_kernel(
    pix_hbm, w_hbm, tile_hbm, row_hbm, day_hbm, out_hbm,
    pix_ref, w_ref, tile_ref, row_ref, day_ref, pos_v, pos_s, src, buf, out_ref, sem, in_sems, out_sems,
):
    loads = [
        pltpu.make_async_copy(a, b, in_sems.at[n])
        for n, (a, b) in enumerate(
            ((row_hbm, row_ref), (tile_hbm, tile_ref), (day_hbm, day_ref), (w_hbm, w_ref), (pix_hbm, pix_ref))
        )
    ]
    for load in loads:
        load.start()
    buf[...] = jnp.zeros_like(buf)
    sub = lax.broadcasted_iota(jnp.int32, (PIX, PIX), 0)
    lane = lax.broadcasted_iota(jnp.int32, (PIX, PIX), 1)
    ahead = jnp.concatenate([jnp.where(sub < lane, 1.0, 0.0), jnp.ones((PIX, PIX), F32)], axis=1).astype(BF16)
    is_w = sub < CAP
    is_row = sub < 2 * CAP
    slot = jnp.where(is_w, sub, jnp.where(is_row, sub - CAP, sub - 2 * CAP))
    for load in loads[:-1]:
        load.wait()
    running = jnp.zeros((PIX, PIX), F32)
    meta = jnp.zeros((PIX, PIX), F32)
    weights = w_ref[...].astype(F32)
    part = (row_ref[...] * 3277) >> 16
    dest_all = part * N_SPACE + tile_ref[...]
    row_all = (row_ref[...] - part * GRID_ROWS).astype(F32)
    day_all = day_ref[...].astype(F32)
    for b in range(BLOCKS):
        dest = dest_all[b : b + 1, :]
        hit = sub == dest
        onehot = jnp.where(hit, 1.0, 0.0).astype(BF16)
        counts = nn(onehot, ahead)
        before = counts[:, :PIX] + running
        running = running + counts[:, PIX:]
        rank = jnp.sum(jnp.where(hit, before, 0.0), axis=0, keepdims=True).astype(jnp.int32)
        value = jnp.where(is_w, weights[b : b + 1, :], jnp.where(is_row, row_all[b : b + 1, :], day_all[b : b + 1, :]))
        column = jnp.where(slot == rank, value, 0.0).astype(BF16)
        meta = meta + nt(onehot, column)
        pos_v[b : b + 1, :] = dest * SLOT + rank
    copy = pltpu.make_async_copy(pos_v, pos_s, sem)
    copy.start()
    loads[-1].wait()
    src[...] = pix_ref[...].astype(F32)
    copy.wait()

    def block(b, carry):
        def some(i, carry):
            for u in range(16):
                at = pos_s[b, i * 16 + u]
                buf[pl.ds(at, 1), :] = src[pl.ds(b * PIX + i * 16 + u, 1), :]
            return carry

        return lax.fori_loop(0, PIX // 16, some, carry)

    lax.fori_loop(0, BLOCKS, block, 0)
    buf[pl.ds(CAP, N_DEV, stride=SLOT), :] = meta

    leaving = []
    for part in range(N_TM):
        blocks = pl.ds(part * N_SPACE, N_SPACE)
        rows = buf[part * KDIM : (part + 1) * KDIM, :]
        out_ref[blocks] = rows.astype(BF16).reshape(N_SPACE, SLOT, PIX)
        leaving.append(pltpu.make_async_copy(out_ref.at[blocks], out_hbm.at[blocks], out_sems.at[part]))
        leaving[-1].start()
    for copy in leaving:
        copy.wait()


def pack(pixels, weights, tile, row, day):
    hbm = pl.BlockSpec(memory_space=pltpu.HBM)
    return pl.pallas_call(
        pack_kernel,
        name="pack_rows",
        out_shape=jax.ShapeDtypeStruct((N_DEV, SLOT, PIX), BF16),
        in_specs=[hbm] * 5,
        out_specs=hbm,
        scratch_shapes=[
            pltpu.VMEM((ROWS, PIX), BF16),
            pltpu.VMEM((BLOCKS, PIX), BF16),
            pltpu.VMEM((BLOCKS, PIX), jnp.int32),
            pltpu.VMEM((BLOCKS, PIX), jnp.int32),
            pltpu.VMEM((BLOCKS, PIX), jnp.int32),
            pltpu.VMEM((BLOCKS, PIX), jnp.int32),
            pltpu.SMEM((BLOCKS, PIX), jnp.int32),
            pltpu.VMEM((ROWS, PIX), F32),
            pltpu.VMEM((N_DEV * SLOT, PIX), F32),
            pltpu.VMEM((N_DEV, SLOT, PIX), BF16),
            pltpu.SemaphoreType.DMA,
            pltpu.SemaphoreType.DMA((5,)),
            pltpu.SemaphoreType.DMA((N_TM,)),
        ],
        compiler_params=pltpu.CompilerParams(vmem_limit_bytes=VMEM_LIMIT),
    )(pixels, *(a.reshape(BLOCKS, PIX) for a in (weights, tile, row, day)))


def me_and_peer():
    me = lax.axis_index("tm") * N_SPACE + lax.axis_index("space")

    def peer(j):
        other = lax.rem(me + j, N_DEV)
        return other, (other // N_SPACE, lax.rem(other, N_SPACE))

    return me, peer


def greet_all(peer):
    barrier = pltpu.get_barrier_semaphore()

    def greet(j, carry):
        pl.semaphore_signal(barrier, inc=1, device_id=peer(j)[1], device_id_type=MESH)
        return carry

    lax.fori_loop(1, N_DEV, greet, 0)
    pl.semaphore_wait(barrier, N_DEV - 1)


G_STEP = 10
HALF = N_DEV // 2


def remote(src, dst, send_sem, recv_sem, device):
    return pltpu.make_async_remote_copy(
        src_ref=src, dst_ref=dst, send_sem=send_sem, recv_sem=recv_sem, device_id=device, device_id_type=MESH
    )


def exchange_kernel(
    x_ref, field_ref, gram_ref, recv, meta_s, onehot_s, flat_s, part_s, pair_s, tiles_s, total_s,
    send_sem, recv_sem, sum_send, sum_recv, out_sems,
):
    tm, space = lax.axis_index("tm"), lax.axis_index("space")
    me, peer = me_and_peer()
    own = pltpu.make_async_copy(x_ref.at[me], recv.at[me], recv_sem.at[0])
    own.start()
    greet_all(peer)

    def send(j, carry):
        stage = j // N_SPACE
        to_tm = lax.rem(tm + stage, N_TM)
        to_space = lax.rem(space + lax.rem(j, N_SPACE), N_SPACE)
        remote(
            x_ref.at[to_tm * N_SPACE + to_space], recv.at[me], send_sem, recv_sem.at[stage], (to_tm, to_space)
        ).start()
        return carry

    lax.fori_loop(1, N_DEV, send, 0)

    lab = lax.broadcasted_iota(jnp.int32, (PIX, KDIM), 0)
    col = lax.broadcasted_iota(jnp.int32, (PIX, KDIM), 1)
    at = col - SLOT * ((col * 1366) >> 16)
    used = at < CAP
    pick_w = jnp.where(used & (lab == at), 1.0, 0.0).astype(BF16)
    pick_t = (
        jnp.where(used & (lab == at + CAP), float(DAY_DEV), 0.0) + jnp.where(used & (lab == at + 2 * CAP), 1.0, 0.0)
    ).astype(BF16)
    from_src = (lax.broadcasted_iota(jnp.int32, (N_SPACE, KDIM), 1) * 1366) >> 16
    mine = from_src == lax.broadcasted_iota(jnp.int32, (N_SPACE, KDIM), 0)
    day = lax.broadcasted_iota(jnp.int32, (DAY_DEV, KDIM), 0).astype(F32)

    def take(stage, carry):
        i = lax.rem(tm + N_TM - stage, N_TM)
        blocks = pl.ds(pl.multiple_of(i * N_SPACE, N_SPACE), N_SPACE)
        remote(x_ref.at[pl.ds(0, N_SPACE)], recv.at[blocks], send_sem, recv_sem.at[stage], (tm, space)).wait_recv()
        meta_s[...] = recv[blocks, SLOT - 16 :, :].astype(F32)[:, 8:, :].reshape(N_SPACE * 8, PIX)
        meta = meta_s[pl.ds(0, N_SPACE, stride=8), :].astype(BF16)
        w_row = jnp.sum(jnp.where(mine, nn(meta, pick_w), 0.0), axis=0, keepdims=True)
        t_row = jnp.sum(jnp.where(mine, nn(meta, pick_t), 0.0), axis=0, keepdims=True)
        pix = recv[blocks].reshape(KDIM, PIX)
        days = pl.ds(pl.multiple_of(i * DAY_DEV, DAY_DEV), DAY_DEV)
        for half in range(GRID_ROWS // G_STEP):
            for u in range(G_STEP):
                g = half * G_STEP + u
                onehot_s[u * DAY_DEV : (u + 1) * DAY_DEV, :] = jnp.where(
                    day == t_row - float(g * DAY_DEV), w_row, 0.0
                ).astype(BF16)
            cells = nn(onehot_s[...], pix).astype(BF16)
            for u in range(G_STEP):
                g = half * G_STEP + u
                block = cells[u * DAY_DEV : (u + 1) * DAY_DEV, :]
                flat_s[days, g * PIX : (g + 1) * PIX] = block
        return carry

    lax.fori_loop(0, N_TM, take, 0)
    leaving = [
        pltpu.make_async_copy(flat_s.at[:, pl.ds(g * PIX, PIX)], field_ref.at[g], out_sems.at[g])
        for g in range(GRID_ROWS)
    ]

    core = lax.rem(tm, 2)
    chip = (tm // 2) * N_SPACE + space
    partner = (tm + 1 - 2 * core, space)

    def half_gram(which):
        rows = flat_s[pl.ds(pl.multiple_of(which * RANK, RANK), RANK), :]
        gram = nt(flat_s[:RANK, :], rows)
        return [gram[:, q * PIX : (q + 1) * PIX].reshape(RANK // 8, 8, PIX) for q in range(2)]

    given = half_gram(1 - core)
    part_s[: HALF // 2] = given[0]
    part_s[HALF // 2 :] = given[1]
    to_pair = remote(part_s, pair_s, sum_send.at[0], sum_recv.at[0], partner)
    to_pair.start()
    for copy in leaving:
        copy.start()
    kept = half_gram(core)
    to_pair.wait_recv()
    pair_s[: HALF // 2] = pair_s[: HALF // 2] + kept[0]
    pair_s[HALF // 2 :] = pair_s[HALF // 2 :] + kept[1]

    def other_chip(j):
        other = lax.rem(chip + j, HALF)
        return other, ((other // N_SPACE) * 2 + core, lax.rem(other, N_SPACE))

    def scatter(j, carry):
        other, device = other_chip(j)
        remote(pair_s.at[other], tiles_s.at[chip], sum_send.at[1], sum_recv.at[1], device).start()
        return carry

    lax.fori_loop(1, HALF, scatter, 0)
    tiles_s[chip] = pair_s[chip]
    scattered = remote(
        pair_s.at[pl.ds(0, HALF - 1)], tiles_s.at[pl.ds(0, HALF - 1)], sum_send.at[1], sum_recv.at[1], partner
    )
    scattered.wait_recv()
    total_s[...] = jnp.sum(tiles_s[...], axis=0)
    place = core * HALF + chip

    def spread(j, carry):
        remote(total_s, gram_ref.at[place], sum_send.at[2], sum_recv.at[2], other_chip(j)[1]).start()
        return carry

    lax.fori_loop(1, HALF, spread, 0)
    gram_ref[place] = total_s[...]
    gathered = remote(
        pair_s.at[pl.ds(0, HALF - 1)], tiles_s.at[pl.ds(0, HALF - 1)], sum_send.at[2], sum_recv.at[2], partner
    )
    gathered.wait_recv()
    my_half = gram_ref.at[pl.ds(core * HALF, HALF)]
    swap = remote(my_half, my_half, sum_send.at[3], sum_recv.at[3], partner)
    swap.start()
    remote(
        x_ref.at[pl.ds(0, N_DEV - 1)], recv.at[pl.ds(0, N_DEV - 1)], send_sem, recv_sem.at[0], partner
    ).wait_send()
    to_pair.wait_send()
    scattered.wait_send()
    gathered.wait_send()
    for copy in leaving:
        copy.wait()
    swap.wait()


def exchange(packed):
    vm = pl.BlockSpec(memory_space=pltpu.VMEM)
    tiles = pltpu.VMEM((HALF, 8, PIX), F32)
    return pl.pallas_call(
        exchange_kernel,
        name="exchange_grid_sum",
        out_shape=(
            jax.ShapeDtypeStruct((GRID_ROWS, DAYS, PIX), BF16),
            jax.ShapeDtypeStruct((N_DEV, 8, PIX), F32),
        ),
        in_specs=[pl.BlockSpec(memory_space=pltpu.HBM)],
        out_specs=(pl.BlockSpec(memory_space=pltpu.HBM), vm),
        scratch_shapes=[
            pltpu.VMEM((N_DEV, SLOT, PIX), BF16),
            pltpu.VMEM((N_SPACE * 8, PIX), F32),
            pltpu.VMEM((G_STEP * DAY_DEV, KDIM), BF16),
            pltpu.VMEM((DAYS, GRID_ROWS * PIX), BF16),
            tiles,
            tiles,
            tiles,
            pltpu.VMEM((8, PIX), F32),
            pltpu.SemaphoreType.DMA,
            pltpu.SemaphoreType.DMA((N_TM,)),
            pltpu.SemaphoreType.DMA((4,)),
            pltpu.SemaphoreType.DMA((4,)),
            pltpu.SemaphoreType.DMA((GRID_ROWS,)),
        ],
        compiler_params=pltpu.CompilerParams(collective_id=0, has_side_effects=True, vmem_limit_bytes=VMEM_LIMIT),
    )(packed)


PANEL = 32


def split2(x):
    high = x.astype(BF16)
    return high, (x - high.astype(F32)).astype(BF16)


def nn3(a, b):
    ah, al = split2(a)
    bh, bl = split2(b)
    return nn(jnp.concatenate([ah, ah, al], axis=1), jnp.concatenate([bh, bl, bh], axis=0))


def nt3(a, b):
    ah, al = split2(a)
    bh, bl = split2(b)
    return nt(jnp.concatenate([ah, ah, al], axis=1), jnp.concatenate([bh, bl, bh], axis=1))


def split3(x):
    high = x.astype(BF16)
    rest = x - high.astype(F32)
    mid = rest.astype(BF16)
    return high, mid, (rest - mid.astype(F32)).astype(BF16)


def dense_kernel(gram_ref, field_in, field_out, basis_out, prop_ref, m_s, v_s, field_ref, basis_ref, sems):
    arriving = pltpu.make_async_copy(field_in, field_ref, sems.at[0])
    arriving.start()
    leaving = pltpu.make_async_copy(field_ref, field_out, sems.at[1])
    lane2 = lax.broadcasted_iota(jnp.int32, (RANK, RANK), 1)
    sub2 = lax.broadcasted_iota(jnp.int32, (RANK, RANK), 0)
    m_s[:, :PIX] = gram_ref[0]
    m_s[:, PIX:RANK] = gram_ref[1]
    m_s[:, RANK:] = jnp.where(lane2 == sub2, 1.0, 0.0)
    sub = lax.broadcasted_iota(jnp.int32, (PANEL, PIX), 0)

    def panel(p, carry):
        start = pl.multiple_of(p * PANEL, PANEL)
        rows = m_s[pl.ds(start, PANEL), :]
        turned = pltpu.roll(rows[:, :RANK], lax.rem(RANK - start, RANK), 1)
        pieces = [turned[:, :PIX]] + [rows[:, q * PIX : (q + 1) * PIX] for q in range(4)]
        scale = jnp.zeros((PANEL, PIX), F32)
        for q in range(PANEL // 8):
            cols = [jnp.broadcast_to(pieces[0][:, q * 8 + k : q * 8 + k + 1], (PANEL, PIX)) for k in range(8)]
            for k in range(8):
                j = q * 8 + k
                pivot = cols[k][j : j + 1, :]
                factor = jnp.where(sub > j, cols[k] * (1.0 / pivot), 0.0)
                scale = jnp.where(sub == j, lax.rsqrt(pivot), scale)
                for kk in range(k + 1, 8):
                    cols[kk] = cols[kk] - factor * cols[kk][j : j + 1, :]
                pieces = [x - factor * x[j : j + 1, :] for x in pieces]
        done = jnp.concatenate([x * scale for x in pieces[1:]], axis=1)
        v_s[pl.ds(start, PANEL), :] = done
        high, mid, low = split3(done)
        left = jnp.concatenate([high, high, mid, mid, high, low], axis=0)[:, :RANK]
        right = jnp.concatenate([high, mid, high, mid, low, high], axis=0)
        m_s[...] = m_s[...] - tn(left, right)
        return carry

    lax.fori_loop(0, RANK // PANEL, panel, 0)
    inv = v_s[:, RANK:]
    scaled = (math.sqrt(CELLS) * inv).astype(BF16)
    arriving.wait()
    leaving.start()
    for g in range(0, GRID_ROWS, 2):
        both = nn(scaled, jnp.concatenate([field_ref[g, :RANK], field_ref[g + 1, :RANK]], axis=1)).astype(BF16)
        basis_ref[g] = both[:, :PIX]
        basis_ref[g + 1] = both[:, PIX:]
    basis_leaving = pltpu.make_async_copy(basis_ref, basis_out, sems.at[2])
    basis_leaving.start()
    first = jnp.where(lane2 >= sub2, v_s[:, :RANK], 0.0)
    second = nn3(inv, jnp.concatenate([gram_ref[2], gram_ref[3]], axis=1))
    factor = jnp.concatenate([first, second], axis=1)
    last = lax.broadcasted_iota(jnp.int32, (RANK, DAYS), 1) == DAYS - 1
    later = jnp.where(last, 0.0, pltpu.roll(factor, DAYS - 1, 1))
    cross = nt3(later, factor)
    polar = cross * (1.0 / jnp.sqrt(jnp.sum(cross * cross) + 1e-06))

    def sweep(i, polar):
        high, low = split2(polar)
        square = nt(jnp.concatenate([high, high, low], axis=1), jnp.concatenate([high, low, high], axis=1))
        s_high, s_low = split2(square)
        cubed = nn(jnp.concatenate([s_high, s_high, s_low], axis=1), jnp.concatenate([high, low, high], axis=0))
        return 1.5 * polar - 0.5 * cubed

    polar = lax.fori_loop(0, ITERS, sweep, polar)
    prop_ref[...] = math.sqrt(RANK) * polar
    leaving.wait()
    basis_leaving.wait()


def dense(gram, field):
    vm = pl.BlockSpec(memory_space=pltpu.VMEM)
    hbm = pl.BlockSpec(memory_space=pltpu.HBM)
    return pl.pallas_call(
        dense_kernel,
        name="dense_algebra",
        out_shape=(
            jax.ShapeDtypeStruct((GRID_ROWS, DAYS, PIX), BF16),
            jax.ShapeDtypeStruct((GRID_ROWS, RANK, PIX), BF16),
            jax.ShapeDtypeStruct((RANK, RANK), F32),
        ),
        in_specs=[vm, hbm],
        out_specs=(hbm, hbm, vm),
        scratch_shapes=[
            pltpu.VMEM((RANK, DAYS), F32),
            pltpu.VMEM((RANK, DAYS), F32),
            pltpu.VMEM((GRID_ROWS, DAYS, PIX), BF16),
            pltpu.VMEM((GRID_ROWS, RANK, PIX), BF16),
            pltpu.SemaphoreType.DMA((3,)),
        ],
        compiler_params=pltpu.CompilerParams(vmem_limit_bytes=VMEM_LIMIT),
    )(gram.reshape(DAYS // PIX, RANK, PIX), field)


def body(pixels, weights, tile_index, tile_row, granule_day):
    packed = pack(pixels, weights, tile_index, tile_row, granule_day)
    field, gram = exchange(packed)
    field, basis, propagator = dense(gram, field)
    return (field[None], basis[None], propagator)


def solution(mesh):
    split = P(("tm", "space"))
    return jax.shard_map(
        body,
        mesh=mesh,
        in_specs=(P(("tm", "space"), None), split, split, split, split),
        out_specs=(P("space", "tm", None, None), P("space", "tm", None, None), P()),
        check_vma=False,
    )
```

```python
import math

import jax
import jax.numpy as jnp
from jax import lax
from jax.experimental import pallas as pl
from jax.experimental.pallas import tpu as pltpu
from jax.sharding import PartitionSpec as P

MESH = pl.DeviceIdType.MESH
GR_DEV = 160
DAYS = 512
RANK = 256
ITERS = 8
PIX = 128
N_TM = 8
N_SPACE = 16
N_DEV = N_TM * N_SPACE
ROWS = 2560
BLOCKS = ROWS // PIX
GRID_ROWS = GR_DEV // N_TM
DAY_DEV = DAYS // N_TM
CAP = 40
SLOT = 48
KDIM = N_SPACE * SLOT
CELLS = N_SPACE * GR_DEV * PIX
VMEM_LIMIT = 62 * 1024 * 1024 + 512 * 1024
F32 = jnp.float32
BF16 = jnp.bfloat16


def nt(a, b):
    return lax.dot_general(a, b, (((1,), (1,)), ((), ())), preferred_element_type=F32)


def tn(a, b):
    return lax.dot_general(a, b, (((0,), (0,)), ((), ())), preferred_element_type=F32)


def nn(a, b):
    return lax.dot_general(a, b, (((1,), (0,)), ((), ())), preferred_element_type=F32)


G_STEP = 10
HALF = N_DEV // 2
GROUP = N_SPACE // 2
WIDE = ROWS + PIX


def remote(src, dst, send_sem, recv_sem, device):
    return pltpu.make_async_remote_copy(
        src_ref=src, dst_ref=dst, send_sem=send_sem, recv_sem=recv_sem, device_id=device, device_id_type=MESH
    )


def message_layout(tile, row, day, weights, pos_s):
    sub = lax.broadcasted_iota(jnp.int32, (PIX, PIX), 0)
    lane = lax.broadcasted_iota(jnp.int32, (PIX, PIX), 1)
    ahead = jnp.concatenate([jnp.where(sub < lane, 1.0, 0.0), jnp.ones((PIX, PIX), F32)], axis=1).astype(BF16)
    is_w = sub < CAP
    is_row = sub < 2 * CAP
    slot = jnp.where(is_w, sub, jnp.where(is_row, sub - CAP, sub - 2 * CAP)).astype(F32)
    part = (row * 3277) >> 16
    dest_all = part * N_SPACE + tile
    row_all = (row - part * GRID_ROWS).astype(F32)
    day_all = day.astype(F32)
    running = jnp.zeros((PIX, PIX), F32)
    meta = jnp.zeros((PIX, PIX), F32)
    for b in range(BLOCKS):
        dest = dest_all[b : b + 1, :]
        hit = sub == dest
        onehot = jnp.where(hit, 1.0, 0.0).astype(BF16)
        counts = nn(onehot, ahead)
        before = counts[:, :PIX] + running
        running = running + counts[:, PIX:]
        rank = jnp.sum(jnp.where(hit, before, 0.0), axis=0, keepdims=True)
        value = jnp.where(is_w, weights[b : b + 1, :], jnp.where(is_row, row_all[b : b + 1, :], day_all[b : b + 1, :]))
        column = jnp.where(slot == rank, value, 0.0).astype(BF16)
        meta = meta + nt(onehot, column)
        pos_s[b : b + 1, :] = (dest * SLOT).astype(F32) + rank
    pos_s[BLOCKS : BLOCKS + 1, :] = (lax.broadcasted_iota(jnp.int32, (1, PIX), 1) * SLOT + CAP).astype(F32)
    return meta


def exchange_kernel(
    pix_hbm, w_hbm, tile_hbm, row_hbm, day_hbm, field_ref, gram_ref,
    pix_s, w_s, tile_s, row_s, day_s, pos_s, pick_s, packed,
    recv, meta_s, onehot_s, flat_s, part_s, pair_s, tiles_s, total_s,
    in_sems, send_sem, recv_sem, sum_send, sum_recv, out_sems,
):
    tm, space = lax.axis_index("tm"), lax.axis_index("space")
    me = tm * N_SPACE + space
    loads = [
        pltpu.make_async_copy(a, b, in_sems.at[n])
        for n, (a, b) in enumerate(
            (
                (row_hbm, row_s),
                (tile_hbm, tile_s),
                (day_hbm, day_s),
                (w_hbm, w_s),
                (pix_hbm, pix_s.at[pl.ds(0, ROWS)]),
            )
        )
    ]
    for load in loads:
        load.start()
    barrier = pltpu.get_barrier_semaphore()

    def greet(j, carry):
        other = lax.rem(me + j, N_DEV)
        device = (other // N_SPACE, lax.rem(other, N_SPACE))
        pl.semaphore_signal(barrier, inc=1, device_id=device, device_id_type=MESH)
        return carry

    lax.fori_loop(1, N_DEV, greet, 0)
    for load in loads[:-1]:
        load.wait()
    meta = message_layout(tile_s[...], row_s[...], day_s[...], w_s[...].astype(F32), pos_s)
    loads[-1].wait()
    pix_s[ROWS:, :] = meta.astype(BF16)
    pl.semaphore_wait(barrier, N_DEV - 1)
    slots = lax.broadcasted_iota(jnp.int32, (GROUP * SLOT, PIX), 0)

    def send(stage, carry):
        to_tm = lax.rem(tm + stage, N_TM)
        for step in range(2):
            half = lax.rem(space // GROUP + step, 2)
            first = to_tm * N_SPACE + half * GROUP
            here = (slots + first * SLOT).astype(F32)
            for b in range(BLOCKS + 1):
                pick_s[step, :, b * PIX : (b + 1) * PIX] = jnp.where(here == pos_s[b : b + 1, :], 1.0, 0.0).astype(BF16)
            rows = nn(pick_s[step], pix_s[...]).astype(BF16)
            packed[pl.ds(first, GROUP)] = rows.reshape(GROUP, SLOT, PIX)
            for j in range(GROUP):
                to_space = half * GROUP + lax.rem(space + j, GROUP)
                block = packed.at[to_tm * N_SPACE + to_space]
                copy = remote(block, recv.at[me], send_sem, recv_sem.at[stage], (to_tm, to_space))
                if step == 0 and j == 0:
                    pl.when(stage > 0)(copy.start)

                    @pl.when(stage == 0)
                    def _():
                        pltpu.make_async_copy(packed.at[me], recv.at[me], recv_sem.at[0]).start()

                else:
                    copy.start()
        return carry

    lax.fori_loop(0, N_TM, send, 0)

    lab = lax.broadcasted_iota(jnp.int32, (PIX, KDIM), 0)
    col = lax.broadcasted_iota(jnp.int32, (PIX, KDIM), 1)
    at = col - SLOT * ((col * 1366) >> 16)
    used = at < CAP
    pick_w = jnp.where(used & (lab == at), 1.0, 0.0).astype(BF16)
    pick_t = (
        jnp.where(used & (lab == at + CAP), float(DAY_DEV), 0.0) + jnp.where(used & (lab == at + 2 * CAP), 1.0, 0.0)
    ).astype(BF16)
    from_src = (lax.broadcasted_iota(jnp.int32, (N_SPACE, KDIM), 1) * 1366) >> 16
    mine = from_src == lax.broadcasted_iota(jnp.int32, (N_SPACE, KDIM), 0)
    day = lax.broadcasted_iota(jnp.int32, (DAY_DEV, KDIM), 0).astype(F32)

    def take(stage, carry):
        i = lax.rem(tm + N_TM - stage, N_TM)
        blocks = pl.ds(pl.multiple_of(i * N_SPACE, N_SPACE), N_SPACE)
        remote(packed.at[pl.ds(0, N_SPACE)], recv.at[blocks], send_sem, recv_sem.at[stage], (tm, space)).wait_recv()
        meta_s[...] = recv[blocks, SLOT - 16 :, :].astype(F32)[:, 8:, :].reshape(N_SPACE * 8, PIX)
        meta = meta_s[pl.ds(0, N_SPACE, stride=8), :].astype(BF16)
        w_row = jnp.sum(jnp.where(mine, nn(meta, pick_w), 0.0), axis=0, keepdims=True)
        t_row = jnp.sum(jnp.where(mine, nn(meta, pick_t), 0.0), axis=0, keepdims=True)
        pix = recv[blocks].reshape(KDIM, PIX)
        days = pl.ds(pl.multiple_of(i * DAY_DEV, DAY_DEV), DAY_DEV)
        for half in range(GRID_ROWS // G_STEP):
            for u in range(G_STEP):
                g = half * G_STEP + u
                onehot_s[u * DAY_DEV : (u + 1) * DAY_DEV, :] = jnp.where(
                    day == t_row - float(g * DAY_DEV), w_row, 0.0
                ).astype(BF16)
            cells = nn(onehot_s[...], pix).astype(BF16)
            for u in range(G_STEP):
                g = half * G_STEP + u
                block = cells[u * DAY_DEV : (u + 1) * DAY_DEV, :]
                flat_s[days, g * PIX : (g + 1) * PIX] = block
        return carry

    lax.fori_loop(0, N_TM, take, 0)
    leaving = [
        pltpu.make_async_copy(flat_s.at[:, pl.ds(g * PIX, PIX)], field_ref.at[g], out_sems.at[g])
        for g in range(GRID_ROWS)
    ]

    core = lax.rem(tm, 2)
    chip = (tm // 2) * N_SPACE + space
    partner = (tm + 1 - 2 * core, space)

    def half_gram(which):
        rows = flat_s[pl.ds(pl.multiple_of(which * RANK, RANK), RANK), :]
        gram = nt(flat_s[:RANK, :], rows)
        return [gram[:, q * PIX : (q + 1) * PIX].reshape(RANK // 8, 8, PIX) for q in range(2)]

    given = half_gram(1 - core)
    part_s[: HALF // 2] = given[0]
    part_s[HALF // 2 :] = given[1]
    to_pair = remote(part_s, pair_s, sum_send.at[0], sum_recv.at[0], partner)
    to_pair.start()
    for copy in leaving:
        copy.start()
    kept = half_gram(core)
    to_pair.wait_recv()
    pair_s[: HALF // 2] = pair_s[: HALF // 2] + kept[0]
    pair_s[HALF // 2 :] = pair_s[HALF // 2 :] + kept[1]

    def other_chip(j):
        other = lax.rem(chip + j, HALF)
        return other, ((other // N_SPACE) * 2 + core, lax.rem(other, N_SPACE))

    def scatter(j, carry):
        other, device = other_chip(j)
        remote(pair_s.at[other], tiles_s.at[chip], sum_send.at[1], sum_recv.at[1], device).start()
        return carry

    lax.fori_loop(1, HALF, scatter, 0)
    tiles_s[chip] = pair_s[chip]
    scattered = remote(
        pair_s.at[pl.ds(0, HALF - 1)], tiles_s.at[pl.ds(0, HALF - 1)], sum_send.at[1], sum_recv.at[1], partner
    )
    scattered.wait_recv()
    total_s[...] = jnp.sum(tiles_s[...], axis=0)
    place = core * HALF + chip

    def spread(j, carry):
        remote(total_s, gram_ref.at[place], sum_send.at[2], sum_recv.at[2], other_chip(j)[1]).start()
        return carry

    lax.fori_loop(1, HALF, spread, 0)
    gram_ref[place] = total_s[...]
    gathered = remote(
        pair_s.at[pl.ds(0, HALF - 1)], tiles_s.at[pl.ds(0, HALF - 1)], sum_send.at[2], sum_recv.at[2], partner
    )
    gathered.wait_recv()
    my_half = gram_ref.at[pl.ds(core * HALF, HALF)]
    swap = remote(my_half, my_half, sum_send.at[3], sum_recv.at[3], partner)
    swap.start()
    remote(
        packed.at[pl.ds(0, N_DEV - 1)], recv.at[pl.ds(0, N_DEV - 1)], send_sem, recv_sem.at[0], partner
    ).wait_send()
    to_pair.wait_send()
    scattered.wait_send()
    gathered.wait_send()
    for copy in leaving:
        copy.wait()
    swap.wait()


def exchange(pixels, weights, tile, row, day):
    vm = pl.BlockSpec(memory_space=pltpu.VMEM)
    tiles = pltpu.VMEM((HALF, 8, PIX), F32)
    return pl.pallas_call(
        exchange_kernel,
        name="exchange_grid_sum",
        out_shape=(
            jax.ShapeDtypeStruct((GRID_ROWS, DAYS, PIX), BF16),
            jax.ShapeDtypeStruct((N_DEV, 8, PIX), F32),
        ),
        in_specs=[pl.BlockSpec(memory_space=pltpu.HBM)] * 5,
        out_specs=(pl.BlockSpec(memory_space=pltpu.HBM), vm),
        scratch_shapes=[
            pltpu.VMEM((WIDE, PIX), BF16),
            pltpu.VMEM((BLOCKS, PIX), BF16),
            pltpu.VMEM((BLOCKS, PIX), jnp.int32),
            pltpu.VMEM((BLOCKS, PIX), jnp.int32),
            pltpu.VMEM((BLOCKS, PIX), jnp.int32),
            pltpu.VMEM((BLOCKS + 1, PIX), F32),
            pltpu.VMEM((2, GROUP * SLOT, WIDE), BF16),
            pltpu.VMEM((N_DEV, SLOT, PIX), BF16),
            pltpu.VMEM((N_DEV, SLOT, PIX), BF16),
            pltpu.VMEM((N_SPACE * 8, PIX), F32),
            pltpu.VMEM((G_STEP * DAY_DEV, KDIM), BF16),
            pltpu.VMEM((DAYS, GRID_ROWS * PIX), BF16),
            tiles,
            tiles,
            tiles,
            pltpu.VMEM((8, PIX), F32),
            pltpu.SemaphoreType.DMA((5,)),
            pltpu.SemaphoreType.DMA,
            pltpu.SemaphoreType.DMA((N_TM,)),
            pltpu.SemaphoreType.DMA((4,)),
            pltpu.SemaphoreType.DMA((4,)),
            pltpu.SemaphoreType.DMA((GRID_ROWS,)),
        ],
        compiler_params=pltpu.CompilerParams(collective_id=0, has_side_effects=True, vmem_limit_bytes=VMEM_LIMIT),
    )(pixels, *(a.reshape(BLOCKS, PIX) for a in (weights, tile, row, day)))


PANEL = 32


def split2(x):
    high = x.astype(BF16)
    return high, (x - high.astype(F32)).astype(BF16)


def nn3(a, b):
    ah, al = split2(a)
    bh, bl = split2(b)
    return nn(jnp.concatenate([ah, ah, al], axis=1), jnp.concatenate([bh, bl, bh], axis=0))


def nt3(a, b):
    ah, al = split2(a)
    bh, bl = split2(b)
    return nt(jnp.concatenate([ah, ah, al], axis=1), jnp.concatenate([bh, bl, bh], axis=1))


def split3(x):
    high = x.astype(BF16)
    rest = x - high.astype(F32)
    mid = rest.astype(BF16)
    return high, mid, (rest - mid.astype(F32)).astype(BF16)


def dense_kernel(gram_ref, field_in, field_out, basis_out, prop_ref, m_s, v_s, field_ref, basis_ref, sems):
    arriving = pltpu.make_async_copy(field_in, field_ref, sems.at[0])
    arriving.start()
    leaving = pltpu.make_async_copy(field_ref, field_out, sems.at[1])
    lane2 = lax.broadcasted_iota(jnp.int32, (RANK, RANK), 1)
    sub2 = lax.broadcasted_iota(jnp.int32, (RANK, RANK), 0)
    m_s[:, :PIX] = gram_ref[0]
    m_s[:, PIX:RANK] = gram_ref[1]
    m_s[:, RANK:] = jnp.where(lane2 == sub2, 1.0, 0.0)
    sub = lax.broadcasted_iota(jnp.int32, (PANEL, PIX), 0)

    def panel(p, carry):
        start = pl.multiple_of(p * PANEL, PANEL)
        rows = m_s[pl.ds(start, PANEL), :]
        turned = pltpu.roll(rows[:, :RANK], lax.rem(RANK - start, RANK), 1)
        pieces = [turned[:, :PIX]] + [rows[:, q * PIX : (q + 1) * PIX] for q in range(4)]
        scale = jnp.zeros((PANEL, PIX), F32)
        for q in range(PANEL // 8):
            cols = [jnp.broadcast_to(pieces[0][:, q * 8 + k : q * 8 + k + 1], (PANEL, PIX)) for k in range(8)]
            for k in range(8):
                j = q * 8 + k
                pivot = cols[k][j : j + 1, :]
                factor = jnp.where(sub > j, cols[k] * (1.0 / pivot), 0.0)
                scale = jnp.where(sub == j, lax.rsqrt(pivot), scale)
                for kk in range(k + 1, 8):
                    cols[kk] = cols[kk] - factor * cols[kk][j : j + 1, :]
                pieces = [x - factor * x[j : j + 1, :] for x in pieces]
        done = jnp.concatenate([x * scale for x in pieces[1:]], axis=1)
        v_s[pl.ds(start, PANEL), :] = done
        high, mid, low = split3(done)
        left = jnp.concatenate([high, high, mid, mid, high, low], axis=0)[:, :RANK]
        right = jnp.concatenate([high, mid, high, mid, low, high], axis=0)
        m_s[...] = m_s[...] - tn(left, right)
        return carry

    lax.fori_loop(0, RANK // PANEL, panel, 0)
    inv = v_s[:, RANK:]
    scaled = (math.sqrt(CELLS) * inv).astype(BF16)
    arriving.wait()
    leaving.start()
    for g in range(0, GRID_ROWS, 2):
        both = nn(scaled, jnp.concatenate([field_ref[g, :RANK], field_ref[g + 1, :RANK]], axis=1)).astype(BF16)
        basis_ref[g] = both[:, :PIX]
        basis_ref[g + 1] = both[:, PIX:]
    basis_leaving = pltpu.make_async_copy(basis_ref, basis_out, sems.at[2])
    basis_leaving.start()
    first = jnp.where(lane2 >= sub2, v_s[:, :RANK], 0.0)
    second = nn3(inv, jnp.concatenate([gram_ref[2], gram_ref[3]], axis=1))
    factor = jnp.concatenate([first, second], axis=1)
    last = lax.broadcasted_iota(jnp.int32, (RANK, DAYS), 1) == DAYS - 1
    later = jnp.where(last, 0.0, pltpu.roll(factor, DAYS - 1, 1))
    cross = nt3(later, factor)
    polar = cross * (1.0 / jnp.sqrt(jnp.sum(cross * cross) + 1e-06))

    def sweep(i, polar):
        high, low = split2(polar)
        square = nt(jnp.concatenate([high, high, low], axis=1), jnp.concatenate([high, low, high], axis=1))
        s_high, s_low = split2(square)
        cubed = nn(jnp.concatenate([s_high, s_high, s_low], axis=1), jnp.concatenate([high, low, high], axis=0))
        return 1.5 * polar - 0.5 * cubed

    polar = lax.fori_loop(0, ITERS, sweep, polar)
    prop_ref[...] = math.sqrt(RANK) * polar
    leaving.wait()
    basis_leaving.wait()


def dense(gram, field):
    vm = pl.BlockSpec(memory_space=pltpu.VMEM)
    hbm = pl.BlockSpec(memory_space=pltpu.HBM)
    return pl.pallas_call(
        dense_kernel,
        name="dense_algebra",
        out_shape=(
            jax.ShapeDtypeStruct((GRID_ROWS, DAYS, PIX), BF16),
            jax.ShapeDtypeStruct((GRID_ROWS, RANK, PIX), BF16),
            jax.ShapeDtypeStruct((RANK, RANK), F32),
        ),
        in_specs=[vm, hbm],
        out_specs=(hbm, hbm, vm),
        scratch_shapes=[
            pltpu.VMEM((RANK, DAYS), F32),
            pltpu.VMEM((RANK, DAYS), F32),
            pltpu.VMEM((GRID_ROWS, DAYS, PIX), BF16),
            pltpu.VMEM((GRID_ROWS, RANK, PIX), BF16),
            pltpu.SemaphoreType.DMA((3,)),
        ],
        compiler_params=pltpu.CompilerParams(vmem_limit_bytes=VMEM_LIMIT),
    )(gram.reshape(DAYS // PIX, RANK, PIX), field)


def body(pixels, weights, tile_index, tile_row, granule_day):
    field, gram = exchange(pixels, weights, tile_index, tile_row, granule_day)
    field, basis, propagator = dense(gram, field)
    return (field[None], basis[None], propagator)


def solution(mesh):
    split = P(("tm", "space"))
    return jax.shard_map(
        body,
        mesh=mesh,
        in_specs=(P(("tm", "space"), None), split, split, split, split),
        out_specs=(P("space", "tm", None, None), P("space", "tm", None, None), P()),
        check_vma=False,
    )
```

```python
import math

import jax
import jax.numpy as jnp
from jax import lax
from jax.experimental import pallas as pl
from jax.experimental.pallas import tpu as pltpu
from jax.sharding import PartitionSpec as P

MESH = pl.DeviceIdType.MESH
GR_DEV = 160
DAYS = 512
RANK = 256
ITERS = 8
PIX = 128
N_TM = 8
N_SPACE = 16
N_DEV = N_TM * N_SPACE
ROWS = 2560
BLOCKS = ROWS // PIX
GRID_ROWS = GR_DEV // N_TM
DAY_DEV = DAYS // N_TM
CAP = 40
SLOT = 48
KDIM = N_SPACE * SLOT
CELLS = N_SPACE * GR_DEV * PIX
VMEM_LIMIT = 62 * 1024 * 1024 + 512 * 1024
F32 = jnp.float32
BF16 = jnp.bfloat16


def nt(a, b):
    return lax.dot_general(a, b, (((1,), (1,)), ((), ())), preferred_element_type=F32)


def tn(a, b):
    return lax.dot_general(a, b, (((0,), (0,)), ((), ())), preferred_element_type=F32)


def nn(a, b):
    return lax.dot_general(a, b, (((1,), (0,)), ((), ())), preferred_element_type=F32)


G_STEP = 10
HALF = N_DEV // 2
GROUP = N_SPACE // 2
WIDE = ROWS + PIX


def remote(src, dst, send_sem, recv_sem, device):
    return pltpu.make_async_remote_copy(
        src_ref=src, dst_ref=dst, send_sem=send_sem, recv_sem=recv_sem, device_id=device, device_id_type=MESH
    )


def message_layout(tile, row, day, weights, pos_s):
    sub = lax.broadcasted_iota(jnp.int32, (PIX, PIX), 0)
    lane = lax.broadcasted_iota(jnp.int32, (PIX, PIX), 1)
    ahead = jnp.concatenate([jnp.where(sub < lane, 1.0, 0.0), jnp.ones((PIX, PIX), F32)], axis=1).astype(BF16)
    is_w = sub < CAP
    is_row = sub < 2 * CAP
    slot = jnp.where(is_w, sub, jnp.where(is_row, sub - CAP, sub - 2 * CAP)).astype(F32)
    part = (row * 3277) >> 16
    dest_all = part * N_SPACE + tile
    row_all = (row - part * GRID_ROWS).astype(F32)
    day_all = day.astype(F32)
    running = jnp.zeros((PIX, PIX), F32)
    meta = jnp.zeros((PIX, PIX), F32)
    for b in range(BLOCKS):
        dest = dest_all[b : b + 1, :]
        hit = sub == dest
        onehot = jnp.where(hit, 1.0, 0.0).astype(BF16)
        counts = nn(onehot, ahead)
        before = counts[:, :PIX] + running
        running = running + counts[:, PIX:]
        rank = jnp.sum(jnp.where(hit, before, 0.0), axis=0, keepdims=True)
        value = jnp.where(is_w, weights[b : b + 1, :], jnp.where(is_row, row_all[b : b + 1, :], day_all[b : b + 1, :]))
        column = jnp.where(slot == rank, value, 0.0).astype(BF16)
        meta = meta + nt(onehot, column)
        pos_s[b : b + 1, :] = (dest * SLOT).astype(F32) + rank
    pos_s[BLOCKS : BLOCKS + 1, :] = (lax.broadcasted_iota(jnp.int32, (1, PIX), 1) * SLOT + CAP).astype(F32)
    return meta


def exchange_kernel(
    pix_hbm, w_hbm, tile_hbm, row_hbm, day_hbm, field_ref, gram_ref,
    pix_s, w_s, tile_s, row_s, day_s, pos_s, pick_s, packed,
    recv, meta_s, onehot_s, flat_s, part_s, pair_s, tiles_s, total_s,
    in_sems, send_sem, recv_sem, sum_send, sum_recv, out_sems, all_in,
):
    tm, space = lax.axis_index("tm"), lax.axis_index("space")
    me = tm * N_SPACE + space
    loads = [
        pltpu.make_async_copy(a, b, in_sems.at[n])
        for n, (a, b) in enumerate(
            (
                (row_hbm, row_s),
                (tile_hbm, tile_s),
                (day_hbm, day_s),
                (w_hbm, w_s),
                (pix_hbm, pix_s.at[pl.ds(0, ROWS)]),
            )
        )
    ]
    for load in loads:
        load.start()
    barrier = pltpu.get_barrier_semaphore()
    row_peers = [(tm, lax.rem(space + j, N_SPACE)) for j in range(1, N_SPACE)]
    column_peers = [(lax.rem(tm + j, N_TM), space) for j in range(1, N_TM)]
    for device in row_peers + column_peers:
        pl.semaphore_signal(barrier, inc=1, device_id=device, device_id_type=MESH)
    for load in loads[:-1]:
        load.wait()
    pl.semaphore_wait(barrier, len(row_peers) + len(column_peers))
    for device in row_peers:
        pl.semaphore_signal(all_in, inc=1, device_id=device, device_id_type=MESH)
    meta = message_layout(tile_s[...], row_s[...], day_s[...], w_s[...].astype(F32), pos_s)
    loads[-1].wait()
    pix_s[ROWS:, :] = meta.astype(BF16)
    pl.semaphore_wait(all_in, len(row_peers))
    slots = lax.broadcasted_iota(jnp.int32, (SLOT, PIX), 0).astype(F32)

    def to_tm_by(stage):
        return lax.rem(stage + N_TM // 2 * lax.rem(tm, 2), N_TM)

    def from_tm_at(stage):
        i = lax.rem(tm + N_TM - stage, N_TM)
        return lax.rem(i + N_TM // 2 * lax.rem(i, 2), N_TM)

    def send(stage, carry):
        ahead = to_tm_by(stage)
        to_tm = lax.rem(tm + ahead, N_TM)
        for step in range(2):
            targets = [lax.rem(space + step * GROUP + j, N_SPACE) for j in range(GROUP)]
            for b in range(BLOCKS + 1):
                place = pos_s[b : b + 1, :]
                for j, to_space in enumerate(targets):
                    here = slots + ((to_tm * N_SPACE + to_space) * SLOT).astype(F32)
                    pick_s[step, j * SLOT : (j + 1) * SLOT, b * PIX : (b + 1) * PIX] = jnp.where(
                        here == place, 1.0, 0.0
                    ).astype(BF16)
            rows = nn(pick_s[step], pix_s[...]).astype(BF16)
            for j, to_space in enumerate(targets):
                to = to_tm * N_SPACE + to_space
                packed[to] = rows[j * SLOT : (j + 1) * SLOT]
                copy = remote(packed.at[to], recv.at[me], send_sem, recv_sem.at[stage], (to_tm, to_space))
                if step == 0 and j == 0:
                    pl.when(ahead > 0)(copy.start)

                    @pl.when(ahead == 0)
                    def _():
                        pltpu.make_async_copy(packed.at[me], recv.at[me], recv_sem.at[stage]).start()

                else:
                    copy.start()
        return carry

    lax.fori_loop(0, N_TM, send, 0)

    lab = lax.broadcasted_iota(jnp.int32, (PIX, KDIM), 0)
    col = lax.broadcasted_iota(jnp.int32, (PIX, KDIM), 1)
    at = col - SLOT * ((col * 1366) >> 16)
    used = at < CAP
    pick_w = jnp.where(used & (lab == at), 1.0, 0.0).astype(BF16)
    pick_t = (
        jnp.where(used & (lab == at + CAP), float(DAY_DEV), 0.0) + jnp.where(used & (lab == at + 2 * CAP), 1.0, 0.0)
    ).astype(BF16)
    from_src = (lax.broadcasted_iota(jnp.int32, (N_SPACE, KDIM), 1) * 1366) >> 16
    mine = from_src == lax.broadcasted_iota(jnp.int32, (N_SPACE, KDIM), 0)
    day = lax.broadcasted_iota(jnp.int32, (DAY_DEV, KDIM), 0).astype(F32)

    def take(stage, carry):
        i = from_tm_at(stage)
        blocks = pl.ds(pl.multiple_of(i * N_SPACE, N_SPACE), N_SPACE)
        remote(packed.at[pl.ds(0, N_SPACE)], recv.at[blocks], send_sem, recv_sem.at[stage], (tm, space)).wait_recv()
        meta_s[...] = recv[blocks, SLOT - 16 :, :].astype(F32)[:, 8:, :].reshape(N_SPACE * 8, PIX)
        meta = meta_s[pl.ds(0, N_SPACE, stride=8), :].astype(BF16)
        w_row = jnp.sum(jnp.where(mine, nn(meta, pick_w), 0.0), axis=0, keepdims=True)
        t_row = jnp.sum(jnp.where(mine, nn(meta, pick_t), 0.0), axis=0, keepdims=True)
        pix = recv[blocks].reshape(KDIM, PIX)
        days = pl.ds(pl.multiple_of(i * DAY_DEV, DAY_DEV), DAY_DEV)
        for half in range(GRID_ROWS // G_STEP):
            for u in range(G_STEP):
                g = half * G_STEP + u
                onehot_s[u * DAY_DEV : (u + 1) * DAY_DEV, :] = jnp.where(
                    day == t_row - float(g * DAY_DEV), w_row, 0.0
                ).astype(BF16)
            cells = nn(onehot_s[...], pix).astype(BF16)
            for u in range(G_STEP):
                g = half * G_STEP + u
                block = cells[u * DAY_DEV : (u + 1) * DAY_DEV, :]
                flat_s[days, g * PIX : (g + 1) * PIX] = block
        return carry

    lax.fori_loop(0, N_TM, take, 0)
    leaving = [
        pltpu.make_async_copy(flat_s.at[:, pl.ds(g * PIX, PIX)], field_ref.at[g], out_sems.at[g])
        for g in range(GRID_ROWS)
    ]

    core = lax.rem(tm, 2)
    chip = (tm // 2) * N_SPACE + space
    partner = (tm + 1 - 2 * core, space)

    def half_gram(which):
        rows = flat_s[pl.ds(pl.multiple_of(which * RANK, RANK), RANK), :]
        gram = nt(flat_s[:RANK, :], rows)
        return [gram[:, q * PIX : (q + 1) * PIX].reshape(RANK // 8, 8, PIX) for q in range(2)]

    given = half_gram(1 - core)
    part_s[: HALF // 2] = given[0]
    part_s[HALF // 2 :] = given[1]
    to_pair = remote(part_s, pair_s, sum_send.at[0], sum_recv.at[0], partner)
    to_pair.start()
    for copy in leaving:
        copy.start()
    kept = half_gram(core)
    to_pair.wait_recv()
    pair_s[: HALF // 2] = pair_s[: HALF // 2] + kept[0]
    pair_s[HALF // 2 :] = pair_s[HALF // 2 :] + kept[1]

    def other_chip(j):
        other = lax.rem(chip + j, HALF)
        return other, ((other // N_SPACE) * 2 + core, lax.rem(other, N_SPACE))

    def scatter(j, carry):
        other, device = other_chip(j)
        remote(pair_s.at[other], tiles_s.at[chip], sum_send.at[1], sum_recv.at[1], device).start()
        return carry

    lax.fori_loop(1, HALF, scatter, 0)
    tiles_s[chip] = pair_s[chip]
    scattered = remote(
        pair_s.at[pl.ds(0, HALF - 1)], tiles_s.at[pl.ds(0, HALF - 1)], sum_send.at[1], sum_recv.at[1], partner
    )
    scattered.wait_recv()
    total_s[...] = jnp.sum(tiles_s[...], axis=0)
    place = core * HALF + chip

    def spread(j, carry):
        remote(total_s, gram_ref.at[place], sum_send.at[2], sum_recv.at[2], other_chip(j)[1]).start()
        return carry

    lax.fori_loop(1, HALF, spread, 0)
    gram_ref[place] = total_s[...]
    gathered = remote(
        pair_s.at[pl.ds(0, HALF - 1)], tiles_s.at[pl.ds(0, HALF - 1)], sum_send.at[2], sum_recv.at[2], partner
    )
    gathered.wait_recv()
    my_half = gram_ref.at[pl.ds(core * HALF, HALF)]
    swap = remote(my_half, my_half, sum_send.at[3], sum_recv.at[3], partner)
    swap.start()
    remote(
        packed.at[pl.ds(0, N_DEV - 1)], recv.at[pl.ds(0, N_DEV - 1)], send_sem, recv_sem.at[0], partner
    ).wait_send()
    to_pair.wait_send()
    scattered.wait_send()
    gathered.wait_send()
    for copy in leaving:
        copy.wait()
    swap.wait()


def exchange(pixels, weights, tile, row, day):
    vm = pl.BlockSpec(memory_space=pltpu.VMEM)
    tiles = pltpu.VMEM((HALF, 8, PIX), F32)
    return pl.pallas_call(
        exchange_kernel,
        name="exchange_grid_sum",
        out_shape=(
            jax.ShapeDtypeStruct((GRID_ROWS, DAYS, PIX), BF16),
            jax.ShapeDtypeStruct((N_DEV, 8, PIX), F32),
        ),
        in_specs=[pl.BlockSpec(memory_space=pltpu.HBM)] * 5,
        out_specs=(pl.BlockSpec(memory_space=pltpu.HBM), vm),
        scratch_shapes=[
            pltpu.VMEM((WIDE, PIX), BF16),
            pltpu.VMEM((BLOCKS, PIX), BF16),
            pltpu.VMEM((BLOCKS, PIX), jnp.int32),
            pltpu.VMEM((BLOCKS, PIX), jnp.int32),
            pltpu.VMEM((BLOCKS, PIX), jnp.int32),
            pltpu.VMEM((BLOCKS + 1, PIX), F32),
            pltpu.VMEM((2, GROUP * SLOT, WIDE), BF16),
            pltpu.VMEM((N_DEV, SLOT, PIX), BF16),
            pltpu.VMEM((N_DEV, SLOT, PIX), BF16),
            pltpu.VMEM((N_SPACE * 8, PIX), F32),
            pltpu.VMEM((G_STEP * DAY_DEV, KDIM), BF16),
            pltpu.VMEM((DAYS, GRID_ROWS * PIX), BF16),
            tiles,
            tiles,
            tiles,
            pltpu.VMEM((8, PIX), F32),
            pltpu.SemaphoreType.DMA((5,)),
            pltpu.SemaphoreType.DMA,
            pltpu.SemaphoreType.DMA((N_TM,)),
            pltpu.SemaphoreType.DMA((4,)),
            pltpu.SemaphoreType.DMA((4,)),
            pltpu.SemaphoreType.DMA((GRID_ROWS,)),
            pltpu.SemaphoreType.REGULAR,
        ],
        compiler_params=pltpu.CompilerParams(collective_id=0, has_side_effects=True, vmem_limit_bytes=VMEM_LIMIT),
    )(pixels, *(a.reshape(BLOCKS, PIX) for a in (weights, tile, row, day)))


PANEL = 32


def split2(x):
    high = x.astype(BF16)
    return high, (x - high.astype(F32)).astype(BF16)


def nn3(a, b):
    ah, al = split2(a)
    bh, bl = split2(b)
    return nn(jnp.concatenate([ah, ah, al], axis=1), jnp.concatenate([bh, bl, bh], axis=0))


def nt3(a, b):
    ah, al = split2(a)
    bh, bl = split2(b)
    return nt(jnp.concatenate([ah, ah, al], axis=1), jnp.concatenate([bh, bl, bh], axis=1))


def split3(x):
    high = x.astype(BF16)
    rest = x - high.astype(F32)
    mid = rest.astype(BF16)
    return high, mid, (rest - mid.astype(F32)).astype(BF16)


def dense_kernel(gram_ref, field_in, field_out, basis_out, prop_ref, m_s, v_s, field_ref, basis_ref, sems):
    arriving = pltpu.make_async_copy(field_in, field_ref, sems.at[0])
    arriving.start()
    leaving = pltpu.make_async_copy(field_ref, field_out, sems.at[1])
    lane2 = lax.broadcasted_iota(jnp.int32, (RANK, RANK), 1)
    sub2 = lax.broadcasted_iota(jnp.int32, (RANK, RANK), 0)
    m_s[:, :PIX] = gram_ref[0]
    m_s[:, PIX:RANK] = gram_ref[1]
    m_s[:, RANK:] = jnp.where(lane2 == sub2, 1.0, 0.0)
    sub = lax.broadcasted_iota(jnp.int32, (PANEL, PIX), 0)

    def panel(p, carry):
        start = pl.multiple_of(p * PANEL, PANEL)
        rows = m_s[pl.ds(start, PANEL), :]
        turned = pltpu.roll(rows[:, :RANK], lax.rem(RANK - start, RANK), 1)
        pieces = [turned[:, :PIX]] + [rows[:, q * PIX : (q + 1) * PIX] for q in range(4)]
        scale = jnp.zeros((PANEL, PIX), F32)
        for q in range(PANEL // 8):
            cols = [jnp.broadcast_to(pieces[0][:, q * 8 + k : q * 8 + k + 1], (PANEL, PIX)) for k in range(8)]
            for k in range(8):
                j = q * 8 + k
                pivot = cols[k][j : j + 1, :]
                factor = jnp.where(sub > j, cols[k] * (1.0 / pivot), 0.0)
                scale = jnp.where(sub == j, lax.rsqrt(pivot), scale)
                for kk in range(k + 1, 8):
                    cols[kk] = cols[kk] - factor * cols[kk][j : j + 1, :]
                pieces = [x - factor * x[j : j + 1, :] for x in pieces]
        done = jnp.concatenate([x * scale for x in pieces[1:]], axis=1)
        v_s[pl.ds(start, PANEL), :] = done
        high, mid, low = split3(done)
        left = jnp.concatenate([high, high, mid, mid, high, low], axis=0)[:, :RANK]
        right = jnp.concatenate([high, mid, high, mid, low, high], axis=0)
        m_s[...] = m_s[...] - tn(left, right)
        return carry

    lax.fori_loop(0, RANK // PANEL, panel, 0)
    inv = v_s[:, RANK:]
    scaled = (math.sqrt(CELLS) * inv).astype(BF16)
    arriving.wait()
    leaving.start()
    for g in range(0, GRID_ROWS, 2):
        both = nn(scaled, jnp.concatenate([field_ref[g, :RANK], field_ref[g + 1, :RANK]], axis=1)).astype(BF16)
        basis_ref[g] = both[:, :PIX]
        basis_ref[g + 1] = both[:, PIX:]
    basis_leaving = pltpu.make_async_copy(basis_ref, basis_out, sems.at[2])
    basis_leaving.start()
    first = jnp.where(lane2 >= sub2, v_s[:, :RANK], 0.0)
    second = nn3(inv, jnp.concatenate([gram_ref[2], gram_ref[3]], axis=1))
    factor = jnp.concatenate([first, second], axis=1)
    last = lax.broadcasted_iota(jnp.int32, (RANK, DAYS), 1) == DAYS - 1
    later = jnp.where(last, 0.0, pltpu.roll(factor, DAYS - 1, 1))
    cross = nt3(later, factor)
    polar = cross * (1.0 / jnp.sqrt(jnp.sum(cross * cross) + 1e-06))

    def sweep(i, polar):
        high, low = split2(polar)
        square = nt(jnp.concatenate([high, high, low], axis=1), jnp.concatenate([high, low, high], axis=1))
        s_high, s_low = split2(square)
        cubed = nn(jnp.concatenate([s_high, s_high, s_low], axis=1), jnp.concatenate([high, low, high], axis=0))
        return 1.5 * polar - 0.5 * cubed

    polar = lax.fori_loop(0, ITERS, sweep, polar)
    prop_ref[...] = math.sqrt(RANK) * polar
    leaving.wait()
    basis_leaving.wait()


def dense(gram, field):
    vm = pl.BlockSpec(memory_space=pltpu.VMEM)
    hbm = pl.BlockSpec(memory_space=pltpu.HBM)
    return pl.pallas_call(
        dense_kernel,
        name="dense_algebra",
        out_shape=(
            jax.ShapeDtypeStruct((GRID_ROWS, DAYS, PIX), BF16),
            jax.ShapeDtypeStruct((GRID_ROWS, RANK, PIX), BF16),
            jax.ShapeDtypeStruct((RANK, RANK), F32),
        ),
        in_specs=[vm, hbm],
        out_specs=(hbm, hbm, vm),
        scratch_shapes=[
            pltpu.VMEM((RANK, DAYS), F32),
            pltpu.VMEM((RANK, DAYS), F32),
            pltpu.VMEM((GRID_ROWS, DAYS, PIX), BF16),
            pltpu.VMEM((GRID_ROWS, RANK, PIX), BF16),
            pltpu.SemaphoreType.DMA((3,)),
        ],
        compiler_params=pltpu.CompilerParams(vmem_limit_bytes=VMEM_LIMIT),
    )(gram.reshape(DAYS // PIX, RANK, PIX), field)


def body(pixels, weights, tile_index, tile_row, granule_day):
    field, gram = exchange(pixels, weights, tile_index, tile_row, granule_day)
    field, basis, propagator = dense(gram, field)
    return (field[None], basis[None], propagator)


def solution(mesh):
    split = P(("tm", "space"))
    return jax.shard_map(
        body,
        mesh=mesh,
        in_specs=(P(("tm", "space"), None), split, split, split, split),
        out_specs=(P("space", "tm", None, None), P("space", "tm", None, None), P()),
        check_vma=False,
    )
```

```python
import math

import jax
import jax.numpy as jnp
from jax import lax
from jax.experimental import pallas as pl
from jax.experimental.pallas import tpu as pltpu
from jax.sharding import PartitionSpec as P

MESH = pl.DeviceIdType.MESH
GR_DEV = 160
DAYS = 512
RANK = 256
ITERS = 8
PIX = 128
N_TM = 8
N_SPACE = 16
N_DEV = N_TM * N_SPACE
ROWS = 2560
BLOCKS = ROWS // PIX
GRID_ROWS = GR_DEV // N_TM
DAY_DEV = DAYS // N_TM
CAP = 40
SLOT = 48
KDIM = N_SPACE * SLOT
CELLS = N_SPACE * GR_DEV * PIX
VMEM_LIMIT = 62 * 1024 * 1024 + 512 * 1024
F32 = jnp.float32
BF16 = jnp.bfloat16


def nt(a, b):
    return lax.dot_general(a, b, (((1,), (1,)), ((), ())), preferred_element_type=F32)


def tn(a, b):
    return lax.dot_general(a, b, (((0,), (0,)), ((), ())), preferred_element_type=F32)


def nn(a, b):
    return lax.dot_general(a, b, (((1,), (0,)), ((), ())), preferred_element_type=F32)


G_STEP = 10
HALF = N_DEV // 2
GROUP = N_SPACE // 2


def remote(src, dst, send_sem, recv_sem, device):
    return pltpu.make_async_remote_copy(
        src_ref=src, dst_ref=dst, send_sem=send_sem, recv_sem=recv_sem, device_id=device, device_id_type=MESH
    )


def message_layout(tile, row, day, weights, pos_s):
    sub = lax.broadcasted_iota(jnp.int32, (PIX, PIX), 0)
    lane = lax.broadcasted_iota(jnp.int32, (PIX, PIX), 1)
    ahead = jnp.concatenate([jnp.where(sub < lane, 1.0, 0.0), jnp.ones((PIX, PIX), F32)], axis=1).astype(BF16)
    is_w = sub < CAP
    is_row = sub < 2 * CAP
    slot = jnp.where(is_w, sub, jnp.where(is_row, sub - CAP, sub - 2 * CAP)).astype(F32)
    part = (row * 3277) >> 16
    dest_all = part * N_SPACE + tile
    row_all = (row - part * GRID_ROWS).astype(F32)
    day_all = day.astype(F32)
    running = jnp.zeros((PIX, PIX), F32)
    meta = jnp.zeros((PIX, PIX), F32)
    for b in range(BLOCKS):
        dest = dest_all[b : b + 1, :]
        hit = sub == dest
        onehot = jnp.where(hit, 1.0, 0.0).astype(BF16)
        counts = nn(onehot, ahead)
        before = counts[:, :PIX] + running
        running = running + counts[:, PIX:]
        rank = jnp.sum(jnp.where(hit, before, 0.0), axis=0, keepdims=True)
        value = jnp.where(is_w, weights[b : b + 1, :], jnp.where(is_row, row_all[b : b + 1, :], day_all[b : b + 1, :]))
        column = jnp.where(slot == rank, value, 0.0).astype(BF16)
        meta = meta + nt(onehot, column)
        pos_s[b : b + 1, :] = (dest * SLOT).astype(F32) + rank
    return meta


def exchange_kernel(
    pix_hbm, w_hbm, tile_hbm, row_hbm, day_hbm, field_ref, gram_ref,
    pix_s, w_s, tile_s, row_s, day_s, pos_s, about_s, pick_s, packed,
    recv, meta_s, onehot_s, flat_s, part_s, pair_s, tiles_s, total_s,
    in_sems, send_sem, recv_sem, sum_send, sum_recv, out_sems, all_in,
):
    tm, space = lax.axis_index("tm"), lax.axis_index("space")
    me = tm * N_SPACE + space
    loads = [
        pltpu.make_async_copy(a, b, in_sems.at[n])
        for n, (a, b) in enumerate(
            (
                (row_hbm, row_s),
                (tile_hbm, tile_s),
                (day_hbm, day_s),
                (w_hbm, w_s),
                (pix_hbm, pix_s),
            )
        )
    ]
    for load in loads:
        load.start()
    barrier = pltpu.get_barrier_semaphore()
    row_peers = [(tm, lax.rem(space + j, N_SPACE)) for j in range(1, N_SPACE)]
    column_peers = [(lax.rem(tm + j, N_TM), space) for j in range(1, N_TM)]
    for device in row_peers + column_peers:
        pl.semaphore_signal(barrier, inc=1, device_id=device, device_id_type=MESH)
    for load in loads[:-1]:
        load.wait()
    pl.semaphore_wait(barrier, len(row_peers) + len(column_peers))
    for device in row_peers:
        pl.semaphore_signal(all_in, inc=1, device_id=device, device_id_type=MESH)
    meta = message_layout(tile_s[...], row_s[...], day_s[...], w_s[...].astype(F32), pos_s)
    loads[-1].wait()
    about_s[...] = jnp.zeros_like(about_s)
    about_s[pl.ds(0, N_DEV, stride=8), :] = meta
    pl.semaphore_wait(all_in, len(row_peers))
    slots = lax.broadcasted_iota(jnp.int32, (CAP, PIX), 0).astype(F32)

    def to_tm_by(stage):
        return lax.rem(stage + N_TM // 2 * lax.rem(tm, 2), N_TM)

    def from_tm_at(stage):
        i = lax.rem(tm + N_TM - stage, N_TM)
        return lax.rem(i + N_TM // 2 * lax.rem(i, 2), N_TM)

    def send(stage, carry):
        ahead = to_tm_by(stage)
        to_tm = lax.rem(tm + ahead, N_TM)
        for step in range(2):
            targets = [lax.rem(space + step * GROUP + j, N_SPACE) for j in range(GROUP)]
            for b in range(BLOCKS):
                place = pos_s[b : b + 1, :]
                for j, to_space in enumerate(targets):
                    here = slots + ((to_tm * N_SPACE + to_space) * SLOT).astype(F32)
                    pick_s[step, j * CAP : (j + 1) * CAP, b * PIX : (b + 1) * PIX] = jnp.where(
                        here == place, 1.0, 0.0
                    ).astype(BF16)
            rows = nn(pick_s[step], pix_s[...])
            for j, to_space in enumerate(targets):
                to = to_tm * N_SPACE + to_space
                last = about_s[pl.ds(pl.multiple_of(to * 8, 8), 8), :]
                packed[to] = jnp.concatenate([rows[j * CAP : (j + 1) * CAP], last], axis=0).astype(BF16)
                copy = remote(packed.at[to], recv.at[me], send_sem, recv_sem.at[stage], (to_tm, to_space))
                if step == 0 and j == 0:
                    pl.when(ahead > 0)(copy.start)

                    @pl.when(ahead == 0)
                    def _():
                        pltpu.make_async_copy(packed.at[me], recv.at[me], recv_sem.at[stage]).start()

                else:
                    copy.start()
        return carry

    lax.fori_loop(0, N_TM, send, 0)

    lab = lax.broadcasted_iota(jnp.int32, (PIX, KDIM), 0)
    col = lax.broadcasted_iota(jnp.int32, (PIX, KDIM), 1)
    at = col - SLOT * ((col * 1366) >> 16)
    used = at < CAP
    pick_w = jnp.where(used & (lab == at), 1.0, 0.0).astype(BF16)
    pick_t = (
        jnp.where(used & (lab == at + CAP), float(DAY_DEV), 0.0) + jnp.where(used & (lab == at + 2 * CAP), 1.0, 0.0)
    ).astype(BF16)
    from_src = (lax.broadcasted_iota(jnp.int32, (N_SPACE, KDIM), 1) * 1366) >> 16
    mine = from_src == lax.broadcasted_iota(jnp.int32, (N_SPACE, KDIM), 0)
    day = lax.broadcasted_iota(jnp.int32, (DAY_DEV, KDIM), 0).astype(F32)

    def take(stage, carry):
        i = from_tm_at(stage)
        blocks = pl.ds(pl.multiple_of(i * N_SPACE, N_SPACE), N_SPACE)
        remote(packed.at[pl.ds(0, N_SPACE)], recv.at[blocks], send_sem, recv_sem.at[stage], (tm, space)).wait_recv()
        meta_s[...] = recv[blocks, SLOT - 16 :, :].astype(F32)[:, 8:, :].reshape(N_SPACE * 8, PIX)
        meta = meta_s[pl.ds(0, N_SPACE, stride=8), :].astype(BF16)
        w_row = jnp.sum(jnp.where(mine, nn(meta, pick_w), 0.0), axis=0, keepdims=True)
        t_row = jnp.sum(jnp.where(mine, nn(meta, pick_t), 0.0), axis=0, keepdims=True)
        pix = recv[blocks].reshape(KDIM, PIX)
        days = pl.ds(pl.multiple_of(i * DAY_DEV, DAY_DEV), DAY_DEV)
        for half in range(GRID_ROWS // G_STEP):
            for u in range(G_STEP):
                g = half * G_STEP + u
                onehot_s[u * DAY_DEV : (u + 1) * DAY_DEV, :] = jnp.where(
                    day == t_row - float(g * DAY_DEV), w_row, 0.0
                ).astype(BF16)
            cells = nn(onehot_s[...], pix).astype(BF16)
            for u in range(G_STEP):
                g = half * G_STEP + u
                block = cells[u * DAY_DEV : (u + 1) * DAY_DEV, :]
                flat_s[days, g * PIX : (g + 1) * PIX] = block
        return carry

    lax.fori_loop(0, N_TM, take, 0)
    leaving = [
        pltpu.make_async_copy(flat_s.at[:, pl.ds(g * PIX, PIX)], field_ref.at[g], out_sems.at[g])
        for g in range(GRID_ROWS)
    ]

    core = lax.rem(tm, 2)
    chip = (tm // 2) * N_SPACE + space
    partner = (tm + 1 - 2 * core, space)

    def half_gram(which):
        rows = flat_s[pl.ds(pl.multiple_of(which * RANK, RANK), RANK), :]
        gram = nt(flat_s[:RANK, :], rows)
        return [gram[:, q * PIX : (q + 1) * PIX].reshape(RANK // 8, 8, PIX) for q in range(2)]

    given = half_gram(1 - core)
    part_s[: HALF // 2] = given[0]
    part_s[HALF // 2 :] = given[1]
    to_pair = remote(part_s, pair_s, sum_send.at[0], sum_recv.at[0], partner)
    to_pair.start()
    for copy in leaving:
        copy.start()
    kept = half_gram(core)
    to_pair.wait_recv()
    pair_s[: HALF // 2] = pair_s[: HALF // 2] + kept[0]
    pair_s[HALF // 2 :] = pair_s[HALF // 2 :] + kept[1]

    def other_chip(j):
        other = lax.rem(chip + j, HALF)
        return other, ((other // N_SPACE) * 2 + core, lax.rem(other, N_SPACE))

    def scatter(j, carry):
        other, device = other_chip(j)
        remote(pair_s.at[other], tiles_s.at[chip], sum_send.at[1], sum_recv.at[1], device).start()
        return carry

    lax.fori_loop(1, HALF, scatter, 0)
    tiles_s[chip] = pair_s[chip]
    scattered = remote(
        pair_s.at[pl.ds(0, HALF - 1)], tiles_s.at[pl.ds(0, HALF - 1)], sum_send.at[1], sum_recv.at[1], partner
    )
    scattered.wait_recv()
    total_s[...] = jnp.sum(tiles_s[...], axis=0)
    place = core * HALF + chip

    def spread(j, carry):
        remote(total_s, gram_ref.at[place], sum_send.at[2], sum_recv.at[2], other_chip(j)[1]).start()
        return carry

    lax.fori_loop(1, HALF, spread, 0)
    gram_ref[place] = total_s[...]
    gathered = remote(
        pair_s.at[pl.ds(0, HALF - 1)], tiles_s.at[pl.ds(0, HALF - 1)], sum_send.at[2], sum_recv.at[2], partner
    )
    gathered.wait_recv()
    my_half = gram_ref.at[pl.ds(core * HALF, HALF)]
    swap = remote(my_half, my_half, sum_send.at[3], sum_recv.at[3], partner)
    swap.start()
    remote(
        packed.at[pl.ds(0, N_DEV - 1)], recv.at[pl.ds(0, N_DEV - 1)], send_sem, recv_sem.at[0], partner
    ).wait_send()
    to_pair.wait_send()
    scattered.wait_send()
    gathered.wait_send()
    for copy in leaving:
        copy.wait()
    swap.wait()


def exchange(pixels, weights, tile, row, day):
    vm = pl.BlockSpec(memory_space=pltpu.VMEM)
    tiles = pltpu.VMEM((HALF, 8, PIX), F32)
    return pl.pallas_call(
        exchange_kernel,
        name="exchange_grid_sum",
        out_shape=(
            jax.ShapeDtypeStruct((GRID_ROWS, DAYS, PIX), BF16),
            jax.ShapeDtypeStruct((N_DEV, 8, PIX), F32),
        ),
        in_specs=[pl.BlockSpec(memory_space=pltpu.HBM)] * 5,
        out_specs=(pl.BlockSpec(memory_space=pltpu.HBM), vm),
        scratch_shapes=[
            pltpu.VMEM((ROWS, PIX), BF16),
            pltpu.VMEM((BLOCKS, PIX), BF16),
            pltpu.VMEM((BLOCKS, PIX), jnp.int32),
            pltpu.VMEM((BLOCKS, PIX), jnp.int32),
            pltpu.VMEM((BLOCKS, PIX), jnp.int32),
            pltpu.VMEM((BLOCKS, PIX), F32),
            pltpu.VMEM((N_DEV * 8, PIX), F32),
            pltpu.VMEM((2, GROUP * CAP, ROWS), BF16),
            pltpu.VMEM((N_DEV, SLOT, PIX), BF16),
            pltpu.VMEM((N_DEV, SLOT, PIX), BF16),
            pltpu.VMEM((N_SPACE * 8, PIX), F32),
            pltpu.VMEM((G_STEP * DAY_DEV, KDIM), BF16),
            pltpu.VMEM((DAYS, GRID_ROWS * PIX), BF16),
            tiles,
            tiles,
            tiles,
            pltpu.VMEM((8, PIX), F32),
            pltpu.SemaphoreType.DMA((5,)),
            pltpu.SemaphoreType.DMA,
            pltpu.SemaphoreType.DMA((N_TM,)),
            pltpu.SemaphoreType.DMA((4,)),
            pltpu.SemaphoreType.DMA((4,)),
            pltpu.SemaphoreType.DMA((GRID_ROWS,)),
            pltpu.SemaphoreType.REGULAR,
        ],
        compiler_params=pltpu.CompilerParams(collective_id=0, has_side_effects=True, vmem_limit_bytes=VMEM_LIMIT),
    )(pixels, *(a.reshape(BLOCKS, PIX) for a in (weights, tile, row, day)))


PANEL = 32


def split2(x):
    high = x.astype(BF16)
    return high, (x - high.astype(F32)).astype(BF16)


def nn3(a, b):
    ah, al = split2(a)
    bh, bl = split2(b)
    return nn(jnp.concatenate([ah, ah, al], axis=1), jnp.concatenate([bh, bl, bh], axis=0))


def nt3(a, b):
    ah, al = split2(a)
    bh, bl = split2(b)
    return nt(jnp.concatenate([ah, ah, al], axis=1), jnp.concatenate([bh, bl, bh], axis=1))


def split3(x):
    high = x.astype(BF16)
    rest = x - high.astype(F32)
    mid = rest.astype(BF16)
    return high, mid, (rest - mid.astype(F32)).astype(BF16)


def dense_kernel(gram_in, field_in, field_out, basis_out, prop_ref, m_s, v_s, field_ref, basis_ref, gram_ref, sems):
    halves = [
        pltpu.make_async_copy(gram_in.at[pl.ds(2 * q, 2)], gram_ref.at[pl.ds(2 * q, 2)], sems.at[3 + q]) for q in range(2)
    ]
    halves[0].start()
    halves[1].start()
    arriving = pltpu.make_async_copy(field_in, field_ref, sems.at[0])
    arriving.start()
    leaving = pltpu.make_async_copy(field_ref, field_out, sems.at[1])
    lane2 = lax.broadcasted_iota(jnp.int32, (RANK, RANK), 1)
    sub2 = lax.broadcasted_iota(jnp.int32, (RANK, RANK), 0)
    m_s[:, RANK:] = jnp.where(lane2 == sub2, 1.0, 0.0)
    halves[0].wait()
    m_s[:, :PIX] = gram_ref[0]
    m_s[:, PIX:RANK] = gram_ref[1]
    sub = lax.broadcasted_iota(jnp.int32, (PANEL, PIX), 0)

    def panel(p, carry):
        start = pl.multiple_of(p * PANEL, PANEL)
        rows = m_s[pl.ds(start, PANEL), :]
        turned = pltpu.roll(rows[:, :RANK], lax.rem(RANK - start, RANK), 1)
        pieces = [turned[:, :PIX]] + [rows[:, q * PIX : (q + 1) * PIX] for q in range(4)]
        scale = jnp.zeros((PANEL, PIX), F32)
        for q in range(PANEL // 8):
            cols = [jnp.broadcast_to(pieces[0][:, q * 8 + k : q * 8 + k + 1], (PANEL, PIX)) for k in range(8)]
            for k in range(8):
                j = q * 8 + k
                pivot = cols[k][j : j + 1, :]
                factor = jnp.where(sub > j, cols[k] * (1.0 / pivot), 0.0)
                scale = jnp.where(sub == j, lax.rsqrt(pivot), scale)
                for kk in range(k + 1, 8):
                    cols[kk] = cols[kk] - factor * cols[kk][j : j + 1, :]
                pieces = [x - factor * x[j : j + 1, :] for x in pieces]
        done = jnp.concatenate([x * scale for x in pieces[1:]], axis=1)
        v_s[pl.ds(start, PANEL), :] = done

        @pl.when(p < RANK // PANEL - 1)
        def _():
            high, mid, low = split3(done)
            left = jnp.concatenate([high, high, mid, mid, high, low], axis=0)[:, :RANK]
            right = jnp.concatenate([high, mid, high, mid, low, high], axis=0)
            m_s[...] = m_s[...] - tn(left, right)

        return carry

    lax.fori_loop(0, RANK // PANEL, panel, 0)
    inv = v_s[:, RANK:]
    scaled = (math.sqrt(CELLS) * inv).astype(BF16)
    arriving.wait()
    leaving.start()
    for g in range(0, GRID_ROWS, 2):
        both = nn(scaled, jnp.concatenate([field_ref[g, :RANK], field_ref[g + 1, :RANK]], axis=1)).astype(BF16)
        basis_ref[g] = both[:, :PIX]
        basis_ref[g + 1] = both[:, PIX:]
    basis_leaving = pltpu.make_async_copy(basis_ref, basis_out, sems.at[2])
    basis_leaving.start()
    first = jnp.where(lane2 >= sub2, v_s[:, :RANK], 0.0)
    halves[1].wait()
    second = nn3(inv, jnp.concatenate([gram_ref[2], gram_ref[3]], axis=1))
    factor = jnp.concatenate([first, second], axis=1)
    last = lax.broadcasted_iota(jnp.int32, (RANK, DAYS), 1) == DAYS - 1
    later = jnp.where(last, 0.0, pltpu.roll(factor, DAYS - 1, 1))
    cross = nt3(later, factor)
    polar = cross * (1.0 / jnp.sqrt(jnp.sum(cross * cross) + 1e-06))

    def sweep(i, polar):
        high, low = split2(polar)
        square = nt(jnp.concatenate([high, high, low], axis=1), jnp.concatenate([high, low, high], axis=1))
        s_high, s_low = split2(square)
        cubed = nn(jnp.concatenate([s_high, s_high, s_low], axis=1), jnp.concatenate([high, low, high], axis=0))
        return 1.5 * polar - 0.5 * cubed

    polar = lax.fori_loop(0, ITERS, sweep, polar, unroll=True)
    prop_ref[...] = math.sqrt(RANK) * polar
    leaving.wait()
    basis_leaving.wait()


def dense(gram, field):
    vm = pl.BlockSpec(memory_space=pltpu.VMEM)
    hbm = pl.BlockSpec(memory_space=pltpu.HBM)
    return pl.pallas_call(
        dense_kernel,
        name="dense_algebra",
        out_shape=(
            jax.ShapeDtypeStruct((GRID_ROWS, DAYS, PIX), BF16),
            jax.ShapeDtypeStruct((GRID_ROWS, RANK, PIX), BF16),
            jax.ShapeDtypeStruct((RANK, RANK), F32),
        ),
        in_specs=[hbm, hbm],
        out_specs=(hbm, hbm, vm),
        scratch_shapes=[
            pltpu.VMEM((RANK, DAYS), F32),
            pltpu.VMEM((RANK, DAYS), F32),
            pltpu.VMEM((GRID_ROWS, DAYS, PIX), BF16),
            pltpu.VMEM((GRID_ROWS, RANK, PIX), BF16),
            pltpu.VMEM((DAYS // PIX, RANK, PIX), F32),
            pltpu.SemaphoreType.DMA((5,)),
        ],
        compiler_params=pltpu.CompilerParams(vmem_limit_bytes=VMEM_LIMIT),
    )(gram.reshape(DAYS // PIX, RANK, PIX), field)


def body(pixels, weights, tile_index, tile_row, granule_day):
    field, gram = exchange(pixels, weights, tile_index, tile_row, granule_day)
    field, basis, propagator = dense(gram, field)
    return (field[None], basis[None], propagator)


def solution(mesh):
    split = P(("tm", "space"))
    return jax.shard_map(
        body,
        mesh=mesh,
        in_specs=(P(("tm", "space"), None), split, split, split, split),
        out_specs=(P("space", "tm", None, None), P("space", "tm", None, None), P()),
        check_vma=False,
    )
```

```python
import math

import jax
import jax.numpy as jnp
from jax import lax
from jax.experimental import pallas as pl
from jax.experimental.pallas import tpu as pltpu
from jax.sharding import PartitionSpec as P

MESH = pl.DeviceIdType.MESH
GR_DEV = 160
DAYS = 512
RANK = 256
ITERS = 8
PIX = 128
N_TM = 8
N_SPACE = 16
N_DEV = N_TM * N_SPACE
ROWS = 2560
BLOCKS = ROWS // PIX
GRID_ROWS = GR_DEV // N_TM
DAY_DEV = DAYS // N_TM
CAP = 40
SLOT = 48
KDIM = N_SPACE * SLOT
CELLS = N_SPACE * GR_DEV * PIX
VMEM_LIMIT = 62 * 1024 * 1024 + 512 * 1024
F32 = jnp.float32
BF16 = jnp.bfloat16


def nt(a, b):
    return lax.dot_general(a, b, (((1,), (1,)), ((), ())), preferred_element_type=F32)


def tn(a, b):
    return lax.dot_general(a, b, (((0,), (0,)), ((), ())), preferred_element_type=F32)


def nn(a, b):
    return lax.dot_general(a, b, (((1,), (0,)), ((), ())), preferred_element_type=F32)


G_STEP = 10
HALF = N_DEV // 2
GROUP = N_SPACE // 2


def remote(src, dst, send_sem, recv_sem, device):
    return pltpu.make_async_remote_copy(
        src_ref=src, dst_ref=dst, send_sem=send_sem, recv_sem=recv_sem, device_id=device, device_id_type=MESH
    )


def message_layout(tile, row, day, weights, pos_s):
    sub = lax.broadcasted_iota(jnp.int32, (PIX, PIX), 0)
    lane = lax.broadcasted_iota(jnp.int32, (PIX, PIX), 1)
    ahead = jnp.concatenate([jnp.where(sub < lane, 1.0, 0.0), jnp.ones((PIX, PIX), F32)], axis=1).astype(BF16)
    is_w = sub < CAP
    is_row = sub < 2 * CAP
    slot = jnp.where(is_w, sub, jnp.where(is_row, sub - CAP, sub - 2 * CAP)).astype(F32)
    part = (row * 3277) >> 16
    dest_all = part * N_SPACE + tile
    row_all = (row - part * GRID_ROWS).astype(F32)
    day_all = day.astype(F32)
    running = jnp.zeros((PIX, PIX), F32)
    meta = jnp.zeros((PIX, PIX), F32)
    for b in range(BLOCKS):
        dest = dest_all[b : b + 1, :]
        hit = sub == dest
        onehot = jnp.where(hit, 1.0, 0.0).astype(BF16)
        counts = nn(onehot, ahead)
        before = counts[:, :PIX] + running
        running = running + counts[:, PIX:]
        rank = jnp.sum(jnp.where(hit, before, 0.0), axis=0, keepdims=True)
        value = jnp.where(is_w, weights[b : b + 1, :], jnp.where(is_row, row_all[b : b + 1, :], day_all[b : b + 1, :]))
        column = jnp.where(slot == rank, value, 0.0).astype(BF16)
        meta = meta + nt(onehot, column)
        pos_s[b : b + 1, :] = (dest * SLOT).astype(F32) + rank
    return meta


def exchange_kernel(
    pix_hbm, w_hbm, tile_hbm, row_hbm, day_hbm, field_ref, gram_out,
    pix_s, w_s, tile_s, row_s, day_s, pos_s, about_s, pick_s, packed,
    gram_ref, recv, meta_s, onehot_s, flat_s, part_s, pair_s, tiles_s, total_s,
    in_sems, send_sem, recv_sem, sum_send, sum_recv, out_sems, all_in,
):
    tm, space = lax.axis_index("tm"), lax.axis_index("space")
    me = tm * N_SPACE + space
    loads = [
        pltpu.make_async_copy(a, b, in_sems.at[n])
        for n, (a, b) in enumerate(
            (
                (row_hbm, row_s),
                (tile_hbm, tile_s),
                (day_hbm, day_s),
                (w_hbm, w_s),
                (pix_hbm, pix_s),
            )
        )
    ]
    for load in loads:
        load.start()
    barrier = pltpu.get_barrier_semaphore()
    row_peers = [(tm, lax.rem(space + j, N_SPACE)) for j in range(1, N_SPACE)]
    column_peers = [(lax.rem(tm + j, N_TM), space) for j in range(1, N_TM)]
    for device in row_peers + column_peers:
        pl.semaphore_signal(barrier, inc=1, device_id=device, device_id_type=MESH)
    for load in loads[:-1]:
        load.wait()
    pl.semaphore_wait(barrier, len(row_peers) + len(column_peers))
    for device in row_peers:
        pl.semaphore_signal(all_in, inc=1, device_id=device, device_id_type=MESH)
    meta = message_layout(tile_s[...], row_s[...], day_s[...], w_s[...].astype(F32), pos_s)
    loads[-1].wait()
    about_s[...] = jnp.zeros_like(about_s)
    about_s[pl.ds(0, N_DEV, stride=8), :] = meta
    pl.semaphore_wait(all_in, len(row_peers))
    slots = lax.broadcasted_iota(jnp.int32, (CAP, PIX), 0).astype(F32)

    def to_tm_by(stage):
        return lax.rem(stage + N_TM // 2 * lax.rem(tm, 2), N_TM)

    def from_tm_at(stage):
        i = lax.rem(tm + N_TM - stage, N_TM)
        return lax.rem(i + N_TM // 2 * lax.rem(i, 2), N_TM)

    def send(stage, carry):
        ahead = to_tm_by(stage)
        to_tm = lax.rem(tm + ahead, N_TM)
        for step in range(2):
            targets = [lax.rem(space + step * GROUP + j, N_SPACE) for j in range(GROUP)]
            for b in range(BLOCKS):
                place = pos_s[b : b + 1, :]
                for j, to_space in enumerate(targets):
                    here = slots + ((to_tm * N_SPACE + to_space) * SLOT).astype(F32)
                    pick_s[step, j * CAP : (j + 1) * CAP, b * PIX : (b + 1) * PIX] = jnp.where(
                        here == place, 1.0, 0.0
                    ).astype(BF16)
            rows = nn(pick_s[step], pix_s[...])
            for j, to_space in enumerate(targets):
                to = to_tm * N_SPACE + to_space
                last = about_s[pl.ds(pl.multiple_of(to * 8, 8), 8), :]
                packed[to] = jnp.concatenate([rows[j * CAP : (j + 1) * CAP], last], axis=0).astype(BF16)
                copy = remote(packed.at[to], recv.at[me], send_sem, recv_sem.at[stage], (to_tm, to_space))
                if step == 0 and j == 0:
                    pl.when(ahead > 0)(copy.start)

                    @pl.when(ahead == 0)
                    def _():
                        pltpu.make_async_copy(packed.at[me], recv.at[me], recv_sem.at[stage]).start()

                else:
                    copy.start()
        return carry

    lax.fori_loop(0, N_TM, send, 0)

    lab = lax.broadcasted_iota(jnp.int32, (PIX, KDIM), 0)
    col = lax.broadcasted_iota(jnp.int32, (PIX, KDIM), 1)
    at = col - SLOT * ((col * 1366) >> 16)
    used = at < CAP
    pick_w = jnp.where(used & (lab == at), 1.0, 0.0).astype(BF16)
    pick_t = (
        jnp.where(used & (lab == at + CAP), float(DAY_DEV), 0.0) + jnp.where(used & (lab == at + 2 * CAP), 1.0, 0.0)
    ).astype(BF16)
    from_src = (lax.broadcasted_iota(jnp.int32, (N_SPACE, KDIM), 1) * 1366) >> 16
    mine = from_src == lax.broadcasted_iota(jnp.int32, (N_SPACE, KDIM), 0)
    day = lax.broadcasted_iota(jnp.int32, (DAY_DEV, KDIM), 0).astype(F32)

    def take(stage, carry):
        i = from_tm_at(stage)
        blocks = pl.ds(pl.multiple_of(i * N_SPACE, N_SPACE), N_SPACE)
        remote(packed.at[pl.ds(0, N_SPACE)], recv.at[blocks], send_sem, recv_sem.at[stage], (tm, space)).wait_recv()
        meta_s[...] = recv[blocks, SLOT - 16 :, :].astype(F32)[:, 8:, :].reshape(N_SPACE * 8, PIX)
        meta = meta_s[pl.ds(0, N_SPACE, stride=8), :].astype(BF16)
        w_row = jnp.sum(jnp.where(mine, nn(meta, pick_w), 0.0), axis=0, keepdims=True)
        t_row = jnp.sum(jnp.where(mine, nn(meta, pick_t), 0.0), axis=0, keepdims=True)
        pix = recv[blocks].reshape(KDIM, PIX)
        days = pl.ds(pl.multiple_of(i * DAY_DEV, DAY_DEV), DAY_DEV)
        for half in range(GRID_ROWS // G_STEP):
            for u in range(G_STEP):
                g = half * G_STEP + u
                onehot_s[u * DAY_DEV : (u + 1) * DAY_DEV, :] = jnp.where(
                    day == t_row - float(g * DAY_DEV), w_row, 0.0
                ).astype(BF16)
            cells = nn(onehot_s[...], pix).astype(BF16)
            for u in range(G_STEP):
                g = half * G_STEP + u
                block = cells[u * DAY_DEV : (u + 1) * DAY_DEV, :]
                flat_s[days, g * PIX : (g + 1) * PIX] = block
        return carry

    lax.fori_loop(0, N_TM, take, 0)
    leaving = [
        pltpu.make_async_copy(flat_s.at[:, pl.ds(g * PIX, PIX)], field_ref.at[g], out_sems.at[g])
        for g in range(GRID_ROWS)
    ]

    core = lax.rem(tm, 2)
    chip = (tm // 2) * N_SPACE + space
    partner = (tm + 1 - 2 * core, space)

    def half_gram(which):
        rows = flat_s[pl.ds(pl.multiple_of(which * RANK, RANK), RANK), :]
        gram = nt(flat_s[:RANK, :], rows)
        return [gram[:, q * PIX : (q + 1) * PIX].reshape(RANK // 8, 8, PIX) for q in range(2)]

    given = half_gram(1 - core)
    part_s[: HALF // 2] = given[0]
    part_s[HALF // 2 :] = given[1]
    to_pair = remote(part_s, pair_s, sum_send.at[0], sum_recv.at[0], partner)
    to_pair.start()
    for copy in leaving:
        copy.start()
    kept = half_gram(core)
    to_pair.wait_recv()
    pair_s[: HALF // 2] = pair_s[: HALF // 2] + kept[0]
    pair_s[HALF // 2 :] = pair_s[HALF // 2 :] + kept[1]

    def to_other_chips(send_one):
        def some(i, carry):
            for u in range(9):
                other = lax.rem(chip + 1 + i * 9 + u, HALF)
                send_one(other, ((other // N_SPACE) * 2 + core, lax.rem(other, N_SPACE)))
            return carry

        lax.fori_loop(0, (HALF - 1) // 9, some, 0)

    def scatter(other, device):
        remote(pair_s.at[other], tiles_s.at[chip], sum_send.at[1], sum_recv.at[1], device).start()

    to_other_chips(scatter)
    tiles_s[chip] = pair_s[chip]
    scattered = remote(
        pair_s.at[pl.ds(0, HALF - 1)], tiles_s.at[pl.ds(0, HALF - 1)], sum_send.at[1], sum_recv.at[1], partner
    )
    scattered.wait_recv()
    total_s[...] = jnp.sum(tiles_s[...], axis=0)
    place = core * HALF + chip

    def spread(other, device):
        remote(total_s, gram_ref.at[place], sum_send.at[2], sum_recv.at[2], device).start()

    to_other_chips(spread)
    gram_ref[place] = total_s[...]
    gathered = remote(
        pair_s.at[pl.ds(0, HALF - 1)], tiles_s.at[pl.ds(0, HALF - 1)], sum_send.at[2], sum_recv.at[2], partner
    )
    gathered.wait_recv()
    my_half = gram_ref.at[pl.ds(core * HALF, HALF)]
    swap = remote(my_half, my_half, sum_send.at[3], sum_recv.at[3], partner)
    swap.start()
    gram_leaving = [
        pltpu.make_async_copy(
            gram_ref.at[pl.ds(which * HALF, HALF)], gram_out.at[pl.ds(which * HALF, HALF)], out_sems.at[GRID_ROWS + n]
        )
        for n, which in enumerate((core, 1 - core))
    ]
    gram_leaving[0].start()
    remote(
        packed.at[pl.ds(0, N_DEV - 1)], recv.at[pl.ds(0, N_DEV - 1)], send_sem, recv_sem.at[0], partner
    ).wait_send()
    to_pair.wait_send()
    scattered.wait_send()
    gathered.wait_send()
    for copy in leaving:
        copy.wait()
    swap.wait_recv()
    gram_leaving[1].start()
    swap.wait_send()
    for copy in gram_leaving:
        copy.wait()


def exchange(pixels, weights, tile, row, day):
    tiles = pltpu.VMEM((HALF, 8, PIX), F32)
    return pl.pallas_call(
        exchange_kernel,
        name="exchange_grid_sum",
        out_shape=(
            jax.ShapeDtypeStruct((GRID_ROWS, DAYS, PIX), BF16),
            jax.ShapeDtypeStruct((N_DEV, 8, PIX), F32),
        ),
        in_specs=[pl.BlockSpec(memory_space=pltpu.HBM)] * 5,
        out_specs=(pl.BlockSpec(memory_space=pltpu.HBM),) * 2,
        scratch_shapes=[
            pltpu.VMEM((ROWS, PIX), BF16),
            pltpu.VMEM((BLOCKS, PIX), BF16),
            pltpu.VMEM((BLOCKS, PIX), jnp.int32),
            pltpu.VMEM((BLOCKS, PIX), jnp.int32),
            pltpu.VMEM((BLOCKS, PIX), jnp.int32),
            pltpu.VMEM((BLOCKS, PIX), F32),
            pltpu.VMEM((N_DEV * 8, PIX), F32),
            pltpu.VMEM((2, GROUP * CAP, ROWS), BF16),
            pltpu.VMEM((N_DEV, SLOT, PIX), BF16),
            pltpu.VMEM((N_DEV, 8, PIX), F32),
            pltpu.VMEM((N_DEV, SLOT, PIX), BF16),
            pltpu.VMEM((N_SPACE * 8, PIX), F32),
            pltpu.VMEM((G_STEP * DAY_DEV, KDIM), BF16),
            pltpu.VMEM((DAYS, GRID_ROWS * PIX), BF16),
            tiles,
            tiles,
            tiles,
            pltpu.VMEM((8, PIX), F32),
            pltpu.SemaphoreType.DMA((5,)),
            pltpu.SemaphoreType.DMA,
            pltpu.SemaphoreType.DMA((N_TM,)),
            pltpu.SemaphoreType.DMA((4,)),
            pltpu.SemaphoreType.DMA((4,)),
            pltpu.SemaphoreType.DMA((GRID_ROWS + 2,)),
            pltpu.SemaphoreType.REGULAR,
        ],
        compiler_params=pltpu.CompilerParams(collective_id=0, has_side_effects=True, vmem_limit_bytes=VMEM_LIMIT),
    )(pixels, *(a.reshape(BLOCKS, PIX) for a in (weights, tile, row, day)))


PANEL = 32


def split2(x):
    high = x.astype(BF16)
    return high, (x - high.astype(F32)).astype(BF16)


def nn3(a, b):
    ah, al = split2(a)
    bh, bl = split2(b)
    return nn(jnp.concatenate([ah, ah, al], axis=1), jnp.concatenate([bh, bl, bh], axis=0))


def nt3(a, b):
    ah, al = split2(a)
    bh, bl = split2(b)
    return nt(jnp.concatenate([ah, ah, al], axis=1), jnp.concatenate([bh, bl, bh], axis=1))


def split3(x):
    high = x.astype(BF16)
    rest = x - high.astype(F32)
    mid = rest.astype(BF16)
    return high, mid, (rest - mid.astype(F32)).astype(BF16)


def dense_kernel(gram_in, field_in, field_out, basis_out, prop_ref, m_s, v_s, field_ref, basis_ref, gram_ref, sems):
    halves = [
        pltpu.make_async_copy(gram_in.at[pl.ds(2 * q, 2)], gram_ref.at[pl.ds(2 * q, 2)], sems.at[3 + q]) for q in range(2)
    ]
    halves[0].start()
    halves[1].start()
    arriving = pltpu.make_async_copy(field_in, field_ref, sems.at[0])
    arriving.start()
    leaving = pltpu.make_async_copy(field_ref, field_out, sems.at[1])
    lane2 = lax.broadcasted_iota(jnp.int32, (RANK, RANK), 1)
    sub2 = lax.broadcasted_iota(jnp.int32, (RANK, RANK), 0)
    m_s[:, RANK:] = jnp.where(lane2 == sub2, 1.0, 0.0)
    halves[0].wait()
    m_s[:, :PIX] = gram_ref[0]
    m_s[:, PIX:RANK] = gram_ref[1]
    sub = lax.broadcasted_iota(jnp.int32, (PANEL, PIX), 0)

    def panel(p, carry):
        start = pl.multiple_of(p * PANEL, PANEL)
        rows = m_s[pl.ds(start, PANEL), :]
        turned = pltpu.roll(rows[:, :RANK], lax.rem(RANK - start, RANK), 1)
        pieces = [turned[:, :PIX]] + [rows[:, q * PIX : (q + 1) * PIX] for q in range(4)]
        scale = jnp.zeros((PANEL, PIX), F32)
        for q in range(PANEL // 8):
            cols = [jnp.broadcast_to(pieces[0][:, q * 8 + k : q * 8 + k + 1], (PANEL, PIX)) for k in range(8)]
            for k in range(8):
                j = q * 8 + k
                pivot = cols[k][j : j + 1, :]
                factor = jnp.where(sub > j, cols[k] * (1.0 / pivot), 0.0)
                scale = jnp.where(sub == j, lax.rsqrt(pivot), scale)
                for kk in range(k + 1, 8):
                    cols[kk] = cols[kk] - factor * cols[kk][j : j + 1, :]
                pieces = [x - factor * x[j : j + 1, :] for x in pieces]
        done = jnp.concatenate([x * scale for x in pieces[1:]], axis=1)
        v_s[pl.ds(start, PANEL), :] = done

        @pl.when(p < RANK // PANEL - 1)
        def _():
            high, mid, low = split3(done)
            left = jnp.concatenate([high, high, mid, mid, high, low], axis=0)[:, :RANK]
            right = jnp.concatenate([high, mid, high, mid, low, high], axis=0)
            m_s[...] = m_s[...] - tn(left, right)

        return carry

    lax.fori_loop(0, RANK // PANEL, panel, 0)
    inv = v_s[:, RANK:]
    scaled = (math.sqrt(CELLS) * inv).astype(BF16)
    arriving.wait()
    leaving.start()
    for g in range(0, GRID_ROWS, 2):
        both = nn(scaled, jnp.concatenate([field_ref[g, :RANK], field_ref[g + 1, :RANK]], axis=1)).astype(BF16)
        basis_ref[g] = both[:, :PIX]
        basis_ref[g + 1] = both[:, PIX:]
    basis_leaving = pltpu.make_async_copy(basis_ref, basis_out, sems.at[2])
    basis_leaving.start()
    first = jnp.where(lane2 >= sub2, v_s[:, :RANK], 0.0)
    halves[1].wait()
    second = nn3(inv, jnp.concatenate([gram_ref[2], gram_ref[3]], axis=1))
    factor = jnp.concatenate([first, second], axis=1)
    last = lax.broadcasted_iota(jnp.int32, (RANK, DAYS), 1) == DAYS - 1
    later = jnp.where(last, 0.0, pltpu.roll(factor, DAYS - 1, 1))
    cross = nt3(later, factor)
    polar = cross * (1.0 / jnp.sqrt(jnp.sum(cross * cross) + 1e-06))

    def sweep(i, polar):
        high, low = split2(polar)
        square = nt(jnp.concatenate([high, high, low], axis=1), jnp.concatenate([high, low, high], axis=1))
        s_high, s_low = split2(square)
        cubed = nn(jnp.concatenate([s_high, s_high, s_low], axis=1), jnp.concatenate([high, low, high], axis=0))
        return 1.5 * polar - 0.5 * cubed

    polar = lax.fori_loop(0, ITERS, sweep, polar, unroll=True)
    prop_ref[...] = math.sqrt(RANK) * polar
    leaving.wait()
    basis_leaving.wait()


def dense(gram, field):
    vm = pl.BlockSpec(memory_space=pltpu.VMEM)
    hbm = pl.BlockSpec(memory_space=pltpu.HBM)
    return pl.pallas_call(
        dense_kernel,
        name="dense_algebra",
        out_shape=(
            jax.ShapeDtypeStruct((GRID_ROWS, DAYS, PIX), BF16),
            jax.ShapeDtypeStruct((GRID_ROWS, RANK, PIX), BF16),
            jax.ShapeDtypeStruct((RANK, RANK), F32),
        ),
        in_specs=[hbm, hbm],
        out_specs=(hbm, hbm, vm),
        scratch_shapes=[
            pltpu.VMEM((RANK, DAYS), F32),
            pltpu.VMEM((RANK, DAYS), F32),
            pltpu.VMEM((GRID_ROWS, DAYS, PIX), BF16),
            pltpu.VMEM((GRID_ROWS, RANK, PIX), BF16),
            pltpu.VMEM((DAYS // PIX, RANK, PIX), F32),
            pltpu.SemaphoreType.DMA((5,)),
        ],
        compiler_params=pltpu.CompilerParams(vmem_limit_bytes=VMEM_LIMIT),
    )(gram.reshape(DAYS // PIX, RANK, PIX), field)


def body(pixels, weights, tile_index, tile_row, granule_day):
    field, gram = exchange(pixels, weights, tile_index, tile_row, granule_day)
    field, basis, propagator = dense(gram, field)
    return (field[None], basis[None], propagator)


def solution(mesh):
    split = P(("tm", "space"))
    return jax.shard_map(
        body,
        mesh=mesh,
        in_specs=(P(("tm", "space"), None), split, split, split, split),
        out_specs=(P("space", "tm", None, None), P("space", "tm", None, None), P()),
        check_vma=False,
    )
```

```python
import math

import jax
import jax.numpy as jnp
from jax import lax
from jax.experimental import pallas as pl
from jax.experimental.pallas import tpu as pltpu
from jax.sharding import PartitionSpec as P

MESH = pl.DeviceIdType.MESH
GR_DEV = 160
DAYS = 512
RANK = 256
ITERS = 8
PIX = 128
N_TM = 8
N_SPACE = 16
N_DEV = N_TM * N_SPACE
ROWS = 2560
BLOCKS = ROWS // PIX
GRID_ROWS = GR_DEV // N_TM
DAY_DEV = DAYS // N_TM
CAP = 40
SLOT = 48
KDIM = N_SPACE * SLOT
CELLS = N_SPACE * GR_DEV * PIX
VMEM_LIMIT = 62 * 1024 * 1024 + 512 * 1024
F32 = jnp.float32
BF16 = jnp.bfloat16


def nt(a, b):
    return lax.dot_general(a, b, (((1,), (1,)), ((), ())), preferred_element_type=F32)


def tn(a, b):
    return lax.dot_general(a, b, (((0,), (0,)), ((), ())), preferred_element_type=F32)


def nn(a, b):
    return lax.dot_general(a, b, (((1,), (0,)), ((), ())), preferred_element_type=F32)


G_STEP = 10
HALF = N_DEV // 2
GROUP = N_SPACE // 2


def remote(src, dst, send_sem, recv_sem, device):
    return pltpu.make_async_remote_copy(
        src_ref=src, dst_ref=dst, send_sem=send_sem, recv_sem=recv_sem, device_id=device, device_id_type=MESH
    )


def message_layout(tile, row, day, weights, pos_s):
    sub = lax.broadcasted_iota(jnp.int32, (PIX, PIX), 0)
    lane = lax.broadcasted_iota(jnp.int32, (PIX, PIX), 1)
    ahead = jnp.concatenate([jnp.where(sub < lane, 1.0, 0.0), jnp.ones((PIX, PIX), F32)], axis=1).astype(BF16)
    is_w = sub < CAP
    is_row = sub < 2 * CAP
    slot = jnp.where(is_w, sub, jnp.where(is_row, sub - CAP, sub - 2 * CAP)).astype(F32)
    part = (row * 3277) >> 16
    dest_all = part * N_SPACE + tile
    row_all = (row - part * GRID_ROWS).astype(F32)
    day_all = day.astype(F32)
    running = jnp.zeros((PIX, PIX), F32)
    meta = jnp.zeros((PIX, PIX), F32)
    for b in range(BLOCKS):
        dest = dest_all[b : b + 1, :]
        hit = sub == dest
        onehot = jnp.where(hit, 1.0, 0.0).astype(BF16)
        counts = nn(onehot, ahead)
        before = counts[:, :PIX] + running
        running = running + counts[:, PIX:]
        rank = jnp.sum(jnp.where(hit, before, 0.0), axis=0, keepdims=True)
        value = jnp.where(is_w, weights[b : b + 1, :], jnp.where(is_row, row_all[b : b + 1, :], day_all[b : b + 1, :]))
        column = jnp.where(slot == rank, value, 0.0).astype(BF16)
        meta = meta + nt(onehot, column)
        pos_s[b : b + 1, :] = (dest * SLOT).astype(F32) + rank
    return meta


def exchange_kernel(
    pix_hbm, w_hbm, tile_hbm, row_hbm, day_hbm, field_ref, gram_out,
    pix_s, w_s, tile_s, row_s, day_s, pos_s, about_s, pick_s, packed,
    gram_ref, recv, meta_s, onehot_s, flat_s, part_s, pair_s, tiles_s, total_s,
    in_sems, send_sem, recv_sem, sum_send, sum_recv, out_sems, all_in,
):
    tm, space = lax.axis_index("tm"), lax.axis_index("space")
    me = tm * N_SPACE + space
    loads = [
        pltpu.make_async_copy(a, b, in_sems.at[n])
        for n, (a, b) in enumerate(
            (
                (row_hbm, row_s),
                (tile_hbm, tile_s),
                (day_hbm, day_s),
                (w_hbm, w_s),
                (pix_hbm, pix_s),
            )
        )
    ]
    for load in loads:
        load.start()
    barrier = pltpu.get_barrier_semaphore()
    row_peers = [(tm, lax.rem(space + j, N_SPACE)) for j in range(1, N_SPACE)]
    column_peers = [(lax.rem(tm + j, N_TM), space) for j in range(1, N_TM)]
    for device in row_peers + column_peers:
        pl.semaphore_signal(barrier, inc=1, device_id=device, device_id_type=MESH)
    for load in loads[:-1]:
        load.wait()
    pl.semaphore_wait(barrier, len(row_peers) + len(column_peers))
    for device in row_peers:
        pl.semaphore_signal(all_in, inc=1, device_id=device, device_id_type=MESH)
    meta = message_layout(tile_s[...], row_s[...], day_s[...], w_s[...].astype(F32), pos_s)
    loads[-1].wait()
    about_s[...] = jnp.zeros_like(about_s)
    about_s[pl.ds(0, N_DEV, stride=8), :] = meta
    pl.semaphore_wait(all_in, len(row_peers))
    slots = lax.broadcasted_iota(jnp.int32, (CAP, PIX), 0).astype(F32)

    def to_tm_by(stage):
        return lax.rem(stage + N_TM // 2 * lax.rem(tm, 2), N_TM)

    def from_tm_at(stage):
        i = lax.rem(tm + N_TM - stage, N_TM)
        return lax.rem(i + N_TM // 2 * lax.rem(i, 2), N_TM)

    def send(stage, carry):
        ahead = to_tm_by(stage)
        to_tm = lax.rem(tm + ahead, N_TM)
        for step in range(2):
            targets = [lax.rem(space + step * GROUP + j, N_SPACE) for j in range(GROUP)]
            for b in range(BLOCKS):
                place = pos_s[b : b + 1, :]
                for j, to_space in enumerate(targets):
                    here = slots + ((to_tm * N_SPACE + to_space) * SLOT).astype(F32)
                    pick_s[step, j * CAP : (j + 1) * CAP, b * PIX : (b + 1) * PIX] = jnp.where(
                        here == place, 1.0, 0.0
                    ).astype(BF16)
            rows = nn(pick_s[step], pix_s[...])
            for j, to_space in enumerate(targets):
                to = to_tm * N_SPACE + to_space
                last = about_s[pl.ds(pl.multiple_of(to * 8, 8), 8), :]
                packed[to] = jnp.concatenate([rows[j * CAP : (j + 1) * CAP], last], axis=0).astype(BF16)
                copy = remote(packed.at[to], recv.at[me], send_sem, recv_sem.at[stage], (to_tm, to_space))
                if step == 0 and j == 0:
                    pl.when(ahead > 0)(copy.start)

                    @pl.when(ahead == 0)
                    def _():
                        pltpu.make_async_copy(packed.at[me], recv.at[me], recv_sem.at[stage]).start()

                else:
                    copy.start()
        return carry

    lax.fori_loop(0, N_TM, send, 0)

    lab = lax.broadcasted_iota(jnp.int32, (PIX, KDIM), 0)
    col = lax.broadcasted_iota(jnp.int32, (PIX, KDIM), 1)
    at = col - SLOT * ((col * 1366) >> 16)
    used = at < CAP
    pick_w = jnp.where(used & (lab == at), 1.0, 0.0).astype(BF16)
    pick_t = (
        jnp.where(used & (lab == at + CAP), float(DAY_DEV), 0.0) + jnp.where(used & (lab == at + 2 * CAP), 1.0, 0.0)
    ).astype(BF16)
    from_src = (lax.broadcasted_iota(jnp.int32, (N_SPACE, KDIM), 1) * 1366) >> 16
    mine = from_src == lax.broadcasted_iota(jnp.int32, (N_SPACE, KDIM), 0)
    day = lax.broadcasted_iota(jnp.int32, (DAY_DEV, KDIM), 0).astype(F32)

    def take(stage, carry):
        i = from_tm_at(stage)
        blocks = pl.ds(pl.multiple_of(i * N_SPACE, N_SPACE), N_SPACE)
        remote(packed.at[pl.ds(0, N_SPACE)], recv.at[blocks], send_sem, recv_sem.at[stage], (tm, space)).wait_recv()
        meta_s[...] = recv[blocks, SLOT - 16 :, :].astype(F32)[:, 8:, :].reshape(N_SPACE * 8, PIX)
        meta = meta_s[pl.ds(0, N_SPACE, stride=8), :].astype(BF16)
        w_row = jnp.sum(jnp.where(mine, nn(meta, pick_w), 0.0), axis=0, keepdims=True)
        t_row = jnp.sum(jnp.where(mine, nn(meta, pick_t), 0.0), axis=0, keepdims=True)
        pix = recv[blocks].reshape(KDIM, PIX)
        days = pl.ds(pl.multiple_of(i * DAY_DEV, DAY_DEV), DAY_DEV)
        for half in range(GRID_ROWS // G_STEP):
            for u in range(G_STEP):
                g = half * G_STEP + u
                onehot_s[u * DAY_DEV : (u + 1) * DAY_DEV, :] = jnp.where(
                    day == t_row - float(g * DAY_DEV), w_row, 0.0
                ).astype(BF16)
            cells = nn(onehot_s[...], pix).astype(BF16)
            for u in range(G_STEP):
                g = half * G_STEP + u
                block = cells[u * DAY_DEV : (u + 1) * DAY_DEV, :]
                flat_s[days, g * PIX : (g + 1) * PIX] = block
        return carry

    lax.fori_loop(0, N_TM, take, 0)
    leaving = [
        pltpu.make_async_copy(flat_s.at[:, pl.ds(g * PIX, PIX)], field_ref.at[g], out_sems.at[g])
        for g in range(GRID_ROWS)
    ]

    core = lax.rem(tm, 2)
    chip = (tm // 2) * N_SPACE + space
    partner = (tm + 1 - 2 * core, space)

    def half_gram(which):
        rows = flat_s[pl.ds(pl.multiple_of(which * RANK, RANK), RANK), :]
        gram = nt(flat_s[:RANK, :], rows)
        return [gram[:, q * PIX : (q + 1) * PIX].reshape(RANK // 8, 8, PIX) for q in range(2)]

    def quarter_gram(which, q):
        rows = flat_s[pl.ds(pl.multiple_of(which * RANK + q * PIX, PIX), PIX), :]
        return nt(flat_s[:RANK, :], rows).reshape(RANK // 8, 8, PIX)

    to_pair = []
    for q in range(2):
        tiles = pl.ds(q * (HALF // 2), HALF // 2)
        part_s[tiles] = quarter_gram(1 - core, q)
        to_pair.append(remote(part_s.at[tiles], pair_s.at[tiles], sum_send.at[4 * q], sum_recv.at[4 * q], partner))
        to_pair[q].start()
    for copy in leaving:
        copy.start()
    kept = half_gram(core)
    for q in range(2):
        tiles = pl.ds(q * (HALF // 2), HALF // 2)
        to_pair[q].wait_recv()
        pair_s[tiles] = pair_s[tiles] + kept[q]

    def to_other_chips(send_one):
        def some(i, carry):
            for u in range(9):
                other = lax.rem(chip + 1 + i * 9 + u, HALF)
                send_one(other, ((other // N_SPACE) * 2 + core, lax.rem(other, N_SPACE)))
            return carry

        lax.fori_loop(0, (HALF - 1) // 9, some, 0)

    def scatter(other, device):
        remote(pair_s.at[other], tiles_s.at[chip], sum_send.at[1], sum_recv.at[1], device).start()

    to_other_chips(scatter)
    tiles_s[chip] = pair_s[chip]
    scattered = remote(
        pair_s.at[pl.ds(0, HALF - 1)], tiles_s.at[pl.ds(0, HALF - 1)], sum_send.at[1], sum_recv.at[1], partner
    )
    scattered.wait_recv()
    total_s[...] = jnp.sum(tiles_s[...], axis=0)
    place = core * HALF + chip

    def spread(other, device):
        remote(total_s, gram_ref.at[place], sum_send.at[2], sum_recv.at[2], device).start()

    to_other_chips(spread)
    gram_ref[place] = total_s[...]
    gathered = remote(
        pair_s.at[pl.ds(0, HALF - 1)], tiles_s.at[pl.ds(0, HALF - 1)], sum_send.at[2], sum_recv.at[2], partner
    )
    gathered.wait_recv()
    my_half = gram_ref.at[pl.ds(core * HALF, HALF)]
    swap = remote(my_half, my_half, sum_send.at[3], sum_recv.at[3], partner)
    swap.start()
    gram_leaving = [
        pltpu.make_async_copy(
            gram_ref.at[pl.ds(which * HALF, HALF)], gram_out.at[pl.ds(which * HALF, HALF)], out_sems.at[GRID_ROWS + n]
        )
        for n, which in enumerate((core, 1 - core))
    ]
    gram_leaving[0].start()
    remote(
        packed.at[pl.ds(0, N_DEV - 1)], recv.at[pl.ds(0, N_DEV - 1)], send_sem, recv_sem.at[0], partner
    ).wait_send()
    for copy in to_pair:
        copy.wait_send()
    scattered.wait_send()
    gathered.wait_send()
    for copy in leaving:
        copy.wait()
    swap.wait_recv()
    gram_leaving[1].start()
    swap.wait_send()
    for copy in gram_leaving:
        copy.wait()


def exchange(pixels, weights, tile, row, day):
    tiles = pltpu.VMEM((HALF, 8, PIX), F32)
    return pl.pallas_call(
        exchange_kernel,
        name="exchange_grid_sum",
        out_shape=(
            jax.ShapeDtypeStruct((GRID_ROWS, DAYS, PIX), BF16),
            jax.ShapeDtypeStruct((N_DEV, 8, PIX), F32),
        ),
        in_specs=[pl.BlockSpec(memory_space=pltpu.HBM)] * 5,
        out_specs=(pl.BlockSpec(memory_space=pltpu.HBM),) * 2,
        scratch_shapes=[
            pltpu.VMEM((ROWS, PIX), BF16),
            pltpu.VMEM((BLOCKS, PIX), BF16),
            pltpu.VMEM((BLOCKS, PIX), jnp.int32),
            pltpu.VMEM((BLOCKS, PIX), jnp.int32),
            pltpu.VMEM((BLOCKS, PIX), jnp.int32),
            pltpu.VMEM((BLOCKS, PIX), F32),
            pltpu.VMEM((N_DEV * 8, PIX), F32),
            pltpu.VMEM((2, GROUP * CAP, ROWS), BF16),
            pltpu.VMEM((N_DEV, SLOT, PIX), BF16),
            pltpu.VMEM((N_DEV, 8, PIX), F32),
            pltpu.VMEM((N_DEV, SLOT, PIX), BF16),
            pltpu.VMEM((N_SPACE * 8, PIX), F32),
            pltpu.VMEM((G_STEP * DAY_DEV, KDIM), BF16),
            pltpu.VMEM((DAYS, GRID_ROWS * PIX), BF16),
            tiles,
            tiles,
            tiles,
            pltpu.VMEM((8, PIX), F32),
            pltpu.SemaphoreType.DMA((5,)),
            pltpu.SemaphoreType.DMA,
            pltpu.SemaphoreType.DMA((N_TM,)),
            pltpu.SemaphoreType.DMA((5,)),
            pltpu.SemaphoreType.DMA((5,)),
            pltpu.SemaphoreType.DMA((GRID_ROWS + 2,)),
            pltpu.SemaphoreType.REGULAR,
        ],
        compiler_params=pltpu.CompilerParams(collective_id=0, has_side_effects=True, vmem_limit_bytes=VMEM_LIMIT),
    )(pixels, *(a.reshape(BLOCKS, PIX) for a in (weights, tile, row, day)))


PANEL = 32


def split2(x):
    high = x.astype(BF16)
    return high, (x - high.astype(F32)).astype(BF16)


def nn3(a, b):
    ah, al = split2(a)
    bh, bl = split2(b)
    return nn(jnp.concatenate([ah, ah, al], axis=1), jnp.concatenate([bh, bl, bh], axis=0))


def nt3(a, b):
    ah, al = split2(a)
    bh, bl = split2(b)
    return nt(jnp.concatenate([ah, ah, al], axis=1), jnp.concatenate([bh, bl, bh], axis=1))


def split3(x):
    high = x.astype(BF16)
    rest = x - high.astype(F32)
    mid = rest.astype(BF16)
    return high, mid, (rest - mid.astype(F32)).astype(BF16)


def dense_kernel(gram_in, field_in, field_out, basis_out, prop_ref, m_s, v_s, field_ref, basis_ref, gram_ref, sems):
    halves = [
        pltpu.make_async_copy(gram_in.at[pl.ds(2 * q, 2)], gram_ref.at[pl.ds(2 * q, 2)], sems.at[3 + q]) for q in range(2)
    ]
    halves[0].start()
    halves[1].start()
    arriving = pltpu.make_async_copy(field_in, field_ref, sems.at[0])
    arriving.start()
    leaving = pltpu.make_async_copy(field_ref, field_out, sems.at[1])
    lane2 = lax.broadcasted_iota(jnp.int32, (RANK, RANK), 1)
    sub2 = lax.broadcasted_iota(jnp.int32, (RANK, RANK), 0)
    m_s[:, RANK:] = jnp.where(lane2 == sub2, 1.0, 0.0)
    halves[0].wait()
    m_s[:, :PIX] = gram_ref[0]
    m_s[:, PIX:RANK] = gram_ref[1]
    sub = lax.broadcasted_iota(jnp.int32, (PANEL, PIX), 0)

    def panel(p, carry):
        start = pl.multiple_of(p * PANEL, PANEL)
        rows = m_s[pl.ds(start, PANEL), :]
        turned = pltpu.roll(rows[:, :RANK], lax.rem(RANK - start, RANK), 1)
        pieces = [turned[:, :PIX]] + [rows[:, q * PIX : (q + 1) * PIX] for q in range(4)]
        scale = jnp.zeros((PANEL, PIX), F32)
        for q in range(PANEL // 8):
            cols = [jnp.broadcast_to(pieces[0][:, q * 8 + k : q * 8 + k + 1], (PANEL, PIX)) for k in range(8)]
            for k in range(8):
                j = q * 8 + k
                pivot = cols[k][j : j + 1, :]
                factor = jnp.where(sub > j, cols[k] * (1.0 / pivot), 0.0)
                scale = jnp.where(sub == j, lax.rsqrt(pivot), scale)
                for kk in range(k + 1, 8):
                    cols[kk] = cols[kk] - factor * cols[kk][j : j + 1, :]
                pieces = [x - factor * x[j : j + 1, :] for x in pieces]
        done = jnp.concatenate([x * scale for x in pieces[1:]], axis=1)
        v_s[pl.ds(start, PANEL), :] = done

        @pl.when(p < RANK // PANEL - 1)
        def _():
            high, mid, low = split3(done)
            left = jnp.concatenate([high, high, mid, mid, high, low], axis=0)[:, :RANK]
            right = jnp.concatenate([high, mid, high, mid, low, high], axis=0)
            m_s[...] = m_s[...] - tn(left, right)

        return carry

    lax.fori_loop(0, RANK // PANEL, panel, 0)
    inv = v_s[:, RANK:]
    scaled = (math.sqrt(CELLS) * inv).astype(BF16)
    arriving.wait()
    leaving.start()
    for g in range(0, GRID_ROWS, 2):
        both = nn(scaled, jnp.concatenate([field_ref[g, :RANK], field_ref[g + 1, :RANK]], axis=1)).astype(BF16)
        basis_ref[g] = both[:, :PIX]
        basis_ref[g + 1] = both[:, PIX:]
    basis_leaving = pltpu.make_async_copy(basis_ref, basis_out, sems.at[2])
    basis_leaving.start()
    first = jnp.where(lane2 >= sub2, v_s[:, :RANK], 0.0)
    halves[1].wait()
    second = nn3(inv, jnp.concatenate([gram_ref[2], gram_ref[3]], axis=1))
    factor = jnp.concatenate([first, second], axis=1)
    last = lax.broadcasted_iota(jnp.int32, (RANK, DAYS), 1) == DAYS - 1
    later = jnp.where(last, 0.0, pltpu.roll(factor, DAYS - 1, 1))
    cross = nt3(later, factor)
    polar = cross * (1.0 / jnp.sqrt(jnp.sum(cross * cross) + 1e-06))

    def sweep(i, polar):
        high, low = split2(polar)
        square = nt(jnp.concatenate([high, high, low], axis=1), jnp.concatenate([high, low, high], axis=1))
        s_high, s_low = split2(square)
        cubed = nn(jnp.concatenate([s_high, s_high, s_low], axis=1), jnp.concatenate([high, low, high], axis=0))
        return 1.5 * polar - 0.5 * cubed

    polar = lax.fori_loop(0, ITERS, sweep, polar, unroll=True)
    prop_ref[...] = math.sqrt(RANK) * polar
    leaving.wait()
    basis_leaving.wait()


def dense(gram, field):
    vm = pl.BlockSpec(memory_space=pltpu.VMEM)
    hbm = pl.BlockSpec(memory_space=pltpu.HBM)
    return pl.pallas_call(
        dense_kernel,
        name="dense_algebra",
        out_shape=(
            jax.ShapeDtypeStruct((GRID_ROWS, DAYS, PIX), BF16),
            jax.ShapeDtypeStruct((GRID_ROWS, RANK, PIX), BF16),
            jax.ShapeDtypeStruct((RANK, RANK), F32),
        ),
        in_specs=[hbm, hbm],
        out_specs=(hbm, hbm, vm),
        scratch_shapes=[
            pltpu.VMEM((RANK, DAYS), F32),
            pltpu.VMEM((RANK, DAYS), F32),
            pltpu.VMEM((GRID_ROWS, DAYS, PIX), BF16),
            pltpu.VMEM((GRID_ROWS, RANK, PIX), BF16),
            pltpu.VMEM((DAYS // PIX, RANK, PIX), F32),
            pltpu.SemaphoreType.DMA((5,)),
        ],
        compiler_params=pltpu.CompilerParams(vmem_limit_bytes=VMEM_LIMIT),
    )(gram.reshape(DAYS // PIX, RANK, PIX), field)


def body(pixels, weights, tile_index, tile_row, granule_day):
    field, gram = exchange(pixels, weights, tile_index, tile_row, granule_day)
    field, basis, propagator = dense(gram, field)
    return (field[None], basis[None], propagator)


def solution(mesh):
    split = P(("tm", "space"))
    return jax.shard_map(
        body,
        mesh=mesh,
        in_specs=(P(("tm", "space"), None), split, split, split, split),
        out_specs=(P("space", "tm", None, None), P("space", "tm", None, None), P()),
        check_vma=False,
    )
```
